128 devices in a mesh: dp: 16 (over y, z), mp: 8 (over x, core).
Axes of the slice: x: 4, y: 4, z: 4, core: 2. Of those that a mesh axis runs over, the one named last changes fastest.
Arguments:
- enc: bfloat16 [4096, 4096], P(('dp', 'mp')), may hold values from -76 to 76
- enc_owner: int32 [4096], P(('dp', 'mp')), may hold values from 0 to 15, as said below
- enc_example: int32 [4096], P(('dp', 'mp')), may hold values from 0 to 7, as said below
- dec: bfloat16 [4096, 4096], P('dp'), may hold values from -36 to 36
- dec_lengths: int32 [16, 8], P('dp'), may hold values from 1 to 64, 256 in all within a row
- norm_gain: bfloat16 [4096], replicated, may hold values from 0.25 to 1.75
- w_query: bfloat16 [4096, 4096], P(None, 'mp'), may hold values from -0.0625 to 0.0625
- w_key: bfloat16 [4096, 4096], P(None, 'mp'), may hold values from -0.0625 to 0.0625
- w_value: bfloat16 [4096, 4096], P(None, 'mp'), may hold values from -0.09375 to 0.09375
- w_out: bfloat16 [4096, 4096], P('mp'), may hold values from -0.09375 to 0.09375
- grad_out: bfloat16 [4096, 4096], P('dp'), may hold values from -12 to 12
Outputs:
- grad_dec: bfloat16 [4096, 4096], P('dp', 'mp')
- grad_enc: bfloat16 [4096, 4096], P(('dp', 'mp'))
- grad_wk: float32 [4096, 4096], P('dp', 'mp')
- grad_wv: float32 [4096, 4096], P('dp', 'mp')
The draws below stay inside these ranges and needn't reach their ends.
Inputs may be any that keep to these rules, and one draw needn't show every extreme that they name: `enc_owner`: each device's 32 encoder rows send at most 4 rows to any one owner and at least one row to every owner; one owner, drawn from the seed, takes exactly 4 rows from every device. `enc_example`: every example of every owner has at least one encoder row. `dec_lengths`: row o holds the lengths of owner o's packed examples in order.
All inputs are finite; a program needn't handle non-finite values.
Results may differ from the reference program's by a relative error of at most 0.025.
The reference program's roundings to bfloat16 on the way count: a program that leaves them out, or rounds other values in their place, can miss the bound.
Values may be sent and summed in bfloat16 or wider, within the bound.
A program may use at most 128 MiB of HBM per device.

```python
import math
import jax
import jax.numpy as jnp
import numpy as np
from jax import lax

D = 4096
HEADS = 16
DH = 256
TGT_DEV = 256
ENC_DEV = 32
EX_OWN = 8
CAP = 4
SLOTS = 512
TGT = 4096
ENC = 4096
N_DP = 16
N_MP = 8


def shared_gauss(key):
    return jax.random.truncated_normal(jax.random.fold_in(key, 900), -4.0, 4.0, (D, HEADS * DH), jnp.float32)


def owner_rows(key):
    key = jax.random.fold_in(key, 902)
    key_full, key_blocks = jax.random.split(key)
    busiest = jax.random.randint(key_full, (), 0, N_DP, dtype=jnp.int32)
    spare = ENC_DEV - CAP - (N_DP - 1)

    def one_block(block_key):
        key_extra, key_order = jax.random.split(block_key)
        extra = jax.random.permutation(key_extra, (N_DP - 1) * (CAP - 1))[:spare] // (CAP - 1)
        others = jnp.concatenate([jnp.arange(N_DP - 1, dtype=jnp.int32), extra.astype(jnp.int32)])
        dest = jnp.concatenate([busiest + jnp.zeros((CAP,), jnp.int32), (busiest + 1 + others) % N_DP])
        return dest[jax.random.permutation(key_order, ENC_DEV)]
    blocks = jax.vmap(one_block)(jax.random.split(key_blocks, N_DP * N_MP))
    return blocks.reshape(-1).astype(jnp.int32)


def draw_enc_owner(key, part):
    return owner_rows(key)


def draw_enc_example(key, part):
    owners = owner_rows(key)
    key = jax.random.fold_in(key, 5)
    key_order, key_rest = jax.random.split(key)
    onehot = (owners[:, None] == jnp.arange(N_DP, dtype=jnp.int32)[None, :]).astype(jnp.int32)
    rank = jnp.sum((jnp.cumsum(onehot, axis=0) - onehot) * onehot, axis=1)
    orders = jax.vmap(lambda order_key: jax.random.permutation(order_key, EX_OWN))(jax.random.split(key_order, N_DP))
    first = orders[owners, jnp.minimum(rank, EX_OWN - 1)]
    rest = jax.random.randint(key_rest, (ENC,), 0, EX_OWN, dtype=jnp.int32)
    return jnp.where(rank < EX_OWN, first, rest).astype(jnp.int32)


def draw_w_query(key, part):
    gauss = shared_gauss(key)
    return (gauss * D ** (-0.5)).astype(jnp.bfloat16)


def draw_w_key(key, part):
    key = jax.random.fold_in(key, 2)
    other = jax.random.truncated_normal(key, -4.0, 4.0, (D, HEADS * DH), jnp.float32)
    mixed = other
    return (mixed * D ** (-0.5)).astype(jnp.bfloat16)


def draw_enc(key, part):
    key = jax.random.fold_in(key, 3)
    key_base = jax.random.fold_in(key, 0)
    base = jax.random.truncated_normal(key_base, -4.0, 4.0, (ENC, D), jnp.float32)
    rows = base
    return rows.astype(jnp.bfloat16)


def draw_dec(key, part):
    key = jax.random.fold_in(key, 4)
    keys = jax.random.split(key, 3)
    column_scale = jnp.exp(jax.random.uniform(keys[0], (D,), jnp.float32, math.log(0.3), math.log(3.0)))
    row_scale = jnp.exp(jax.random.uniform(keys[1], (TGT, 1), jnp.float32, math.log(0.3), math.log(3.0)))
    rows = jax.random.truncated_normal(keys[2], -4.0, 4.0, (TGT, D), jnp.float32) * row_scale * column_scale[None, :]
    return rows.astype(jnp.bfloat16)


def levels(key, dims, cuts, smallest, largest):
    def one(position, shards_of):
        steps = jax.random.uniform(jax.random.fold_in(jax.random.fold_in(key, 6), position), (shards_of,), jnp.float32, smallest / len(cuts), largest / len(cuts))
        return jnp.repeat(jnp.exp(steps), dims[position] // shards_of).reshape((-1,) + (1,) * (len(dims) - position - 1))

    level = one(*cuts[0])
    for cut in cuts[1:]:
        level = level * one(*cut)
    return level


def profile(count, total, limit, skew):
    loads = [(1 << 20) // math.isqrt(grade ** skew) + 1 for grade in range(2, count + 1)]
    surplus, given = total - limit - (count - 1), [1] * (count - 1)
    while surplus > 0:
        free = [i for i in range(count - 1) if given[i] < limit]
        pool, budget = sum([loads[i] for i in free]), surplus
        for i in free:
            more = min(limit - given[i], max(1, budget * loads[i] // pool), surplus)
            given[i] = given[i] + more
            surplus = surplus - more
    return np.array([limit] + given)


def uneven_parts(stream_key, amount, total, limit, lean):
    if amount == 2:
        one = jax.random.randint(stream_key, (), max(1, total - limit), min(limit, total - 1) + 1)
        return jnp.stack([one, total - one])
    lengths = jnp.asarray(profile(amount, total, limit, lean), jnp.int32)
    twos = (amount - 1) // 2
    source_of, receiver = lengths[1:1 + 2 * twos:2], lengths[2:2 + 2 * twos:2]
    slack = jnp.minimum(source_of - 1, limit - receiver)
    shifted = jax.random.randint(jax.random.fold_in(stream_key, 1), (twos,), 0, 1 << 20) % (slack + 1)
    lengths = lengths.at[1:1 + 2 * twos:2].set(source_of - shifted).at[2:2 + 2 * twos:2].set(receiver + shifted)
    return lengths[jax.random.permutation(jax.random.fold_in(stream_key, 2), amount)]


def gaussian(own_key, extent, scale, limit, pieces=(), kind=jnp.bfloat16):
    entries = jax.random.normal(own_key, extent, jnp.float32) * scale
    if len(pieces) > 0:
        entries = levels(own_key, extent, pieces, -0.22, 0.18) * entries
    return jnp.clip(entries, min=-limit, max=limit).astype(kind)


def setup_inputs(seed: int = 0) -> dict:
    key_of = jax.random.split(jax.random.key(seed), 12)
    enc = draw_enc(jax.random.fold_in(key_of[11], 71), 0)
    enc_owner = draw_enc_owner(jax.random.fold_in(key_of[11], 71), 0)
    enc_example = draw_enc_example(jax.random.fold_in(key_of[11], 71), 0)
    dec = draw_dec(jax.random.fold_in(key_of[11], 71), 0)
    dec_lengths = jax.vmap(lambda own: uneven_parts(own, EX_OWN, TGT_DEV, TGT_DEV // 4, 1))(jax.random.split(key_of[4], N_DP)).reshape((N_DP, EX_OWN)).astype(jnp.int32)
    norm_gain = jnp.clip(1.0 + 0.15 * jax.random.normal(key_of[5], (D,), jnp.float32), 0.25, 1.75).astype(jnp.bfloat16)
    w_query = draw_w_query(jax.random.fold_in(key_of[11], 71), 0)
    w_key = draw_w_key(jax.random.fold_in(key_of[11], 71), 0)
    w_value = gaussian(key_of[8], (D, HEADS * DH), D ** -0.5, 0.09375, ((1, 8),))
    w_out = gaussian(key_of[9], (HEADS * DH, D), (HEADS * DH) ** -0.5, 0.09375, ((0, 8),))
    grad_out = gaussian(key_of[10], (TGT, D), 3.0, 12.0, ((0, 16),))
    return dict(enc=enc, enc_owner=enc_owner, enc_example=enc_example, dec=dec, dec_lengths=dec_lengths, norm_gain=norm_gain, w_query=w_query, w_key=w_key, w_value=w_value, w_out=w_out, grad_out=grad_out)


def settle(values):
    return lax.optimization_barrier(values.astype(jnp.bfloat16)).astype(jnp.float32)

def attention_grads(query_rows, grad_rows, key_rows, value_rows, segment, slot_example):
    tgt_rows = query_rows.shape[0]
    slot_count = key_rows.shape[0]
    head_count = query_rows.shape[1] // DH
    score_scale = DH ** (-0.5)
    query_heads = query_rows.astype(jnp.float32).reshape(tgt_rows, head_count, DH)
    grad_heads = grad_rows.astype(jnp.float32).reshape(tgt_rows, head_count, DH)
    key_heads = key_rows.astype(jnp.float32).reshape(slot_count, head_count, DH)
    value_heads = value_rows.astype(jnp.float32).reshape(slot_count, head_count, DH)
    scores = jnp.einsum('thd,shd->hts', query_heads, key_heads) * score_scale
    allowed = (segment[:, None] == slot_example[None, :])[None, :, :]
    scores = jnp.where(allowed, scores, -1e+30)
    row_max = lax.optimization_barrier(jnp.max(scores, axis=-1, keepdims=True))
    raw_weights = jnp.where(allowed, jnp.exp(scores - row_max), 0.0)
    probs_wide = raw_weights / lax.optimization_barrier(jnp.sum(raw_weights, axis=-1, keepdims=True))
    probs_narrow = settle(probs_wide)
    grad_probs = jnp.einsum('thd,shd->hts', grad_heads, value_heads)
    inner_sum = lax.optimization_barrier(jnp.sum(probs_wide * grad_probs, axis=-1, keepdims=True))
    grad_scores = settle(probs_wide * (grad_probs - inner_sum) * score_scale)
    grad_query = jnp.einsum('hts,shd->thd', grad_scores, key_heads).astype(jnp.bfloat16)
    grad_key = jnp.einsum('hts,thd->shd', grad_scores, query_heads).astype(jnp.bfloat16)
    grad_value = jnp.einsum('hts,thd->shd', probs_narrow, grad_heads).astype(jnp.bfloat16)
    return (grad_query.reshape(tgt_rows, -1), grad_key.reshape(slot_count, -1), grad_value.reshape(slot_count, -1))

def reference(enc, enc_owner, enc_example, dec, dec_lengths, norm_gain, w_query, w_key, w_value, w_out, grad_out):
    dec_wide = dec.astype(jnp.float32)
    root_mean = jnp.sqrt(lax.optimization_barrier(jnp.mean(dec_wide * dec_wide, axis=-1, keepdims=True)) + 1e-06)
    unit_rows = dec_wide / root_mean
    gain_wide = norm_gain.astype(jnp.float32)
    normed = (unit_rows * gain_wide[None, :]).astype(jnp.bfloat16)
    query_rows = jnp.dot(normed, w_query, preferred_element_type=jnp.float32).astype(jnp.bfloat16)
    key_rows = jnp.dot(enc, w_key, preferred_element_type=jnp.float32).astype(jnp.bfloat16)
    value_rows = jnp.dot(enc, w_value, preferred_element_type=jnp.float32).astype(jnp.bfloat16)
    grad_context = jnp.dot(grad_out, w_out.T, preferred_element_type=jnp.float32).astype(jnp.bfloat16)
    total_rows = enc.shape[0]
    proj_width = HEADS * DH
    owner_ids = jnp.arange(N_DP, dtype=jnp.int32)
    onehot = (enc_owner[:, None] == owner_ids[None, :]).astype(jnp.int32)
    rank = lax.optimization_barrier(jnp.sum((jnp.cumsum(onehot, axis=0) - onehot) * onehot, axis=1)).astype(jnp.int32)
    table = jnp.full((N_DP, SLOTS), total_rows, jnp.int32)
    table = table.at[enc_owner, rank].set(jnp.arange(total_rows, dtype=jnp.int32))
    bounds = jnp.cumsum(dec_lengths, axis=1)
    places = jnp.arange(TGT_DEV, dtype=jnp.int32)
    segment = lax.optimization_barrier(jnp.sum((bounds[:, None, :] <= places[None, :, None]).astype(jnp.int32), axis=-1)).astype(jnp.int32)

    def owner_step(items):
        query_part, grad_part, segment_part, index_part = items
        valid = index_part < total_rows
        safe = jnp.minimum(index_part, total_rows - 1).astype(jnp.int32)
        slot_example = jnp.where(valid, enc_example[safe], -1).astype(jnp.int32)
        return attention_grads(query_part, grad_part, key_rows[safe], value_rows[safe], segment_part, slot_example)
    grad_query, grad_key, grad_value = lax.map(owner_step, (query_rows.reshape(N_DP, TGT_DEV, proj_width), grad_context.reshape(N_DP, TGT_DEV, proj_width), segment, table))
    flat_index = table.reshape(-1)
    key_grads = jnp.zeros((total_rows + 1, proj_width), jnp.bfloat16)
    key_grads = key_grads.at[flat_index].set(grad_key.reshape(-1, proj_width))[:total_rows]
    value_grads = jnp.zeros((total_rows + 1, proj_width), jnp.bfloat16)
    value_grads = value_grads.at[flat_index].set(grad_value.reshape(-1, proj_width))[:total_rows]
    group_width = proj_width // N_MP
    enc_total = jnp.zeros(enc.shape, jnp.float32)
    for group in range(N_MP):
        low = group * group_width
        high = low + group_width
        term = jnp.dot(key_grads[:, low:high], w_key[:, low:high].T, preferred_element_type=jnp.float32)
        term = term + jnp.dot(value_grads[:, low:high], w_value[:, low:high].T, preferred_element_type=jnp.float32)
        enc_total = enc_total + settle(term)
    grad_enc = enc_total.astype(jnp.bfloat16)
    grad_wk = jnp.dot(enc.T, key_grads, preferred_element_type=jnp.float32)
    grad_wv = jnp.dot(enc.T, value_grads, preferred_element_type=jnp.float32)
    grad_normed = jnp.dot(grad_query.reshape(-1, proj_width), w_query.T, preferred_element_type=jnp.float32)
    scaled = grad_normed * gain_wide[None, :]
    inner_mean = lax.optimization_barrier(jnp.mean(scaled * unit_rows, axis=-1, keepdims=True))
    grad_dec = ((scaled - unit_rows * inner_mean) / root_mean).astype(jnp.bfloat16)
    return (grad_dec, grad_enc, grad_wk, grad_wv)
```

```python
import functools

import jax
import jax.numpy as jnp
from jax import lax
from jax.experimental import pallas as pl
from jax.experimental.pallas import tpu as pltpu
from jax.sharding import PartitionSpec as P

MESH = pl.DeviceIdType.MESH
BF = jnp.bfloat16
F32 = jnp.float32
DH = 256
D = 4096
NT = (((1,), (1,)), ((), ()))
TN = (((0,), (0,)), ((), ()))


def dot(a, b):
    return jnp.dot(a, b, preferred_element_type=F32)


def dot_nt(a, b):
    return lax.dot_general(a, b, NT, preferred_element_type=F32)


def dot_tn(a, b):
    return lax.dot_general(a, b, TN, preferred_element_type=F32)


def add4(value, step):
    return lax.rem(value + step, 4)


def kernel(
    enc_ref,
    info_ref,
    len_ref,
    gain_ref,
    dec_hbm,
    go_hbm,
    wq_hbm,
    wk_hbm,
    wv_hbm,
    wo_hbm,
    gd_ref,
    ge_ref,
    gwk_ref,
    gwv_ref,
    dec_v,
    go_v,
    wq_v,
    wk_v,
    wv_v,
    wo_v,
    enc_all,
    normed,
    rms_v,
    info_all,
    q_v,
    gc_v,
    gq_v,
    place_t,
    kv0_s,
    kv1_s,
    kv0_r,
    kv1_r,
    ret_s,
    ret_r,
    g_own,
    g_all,
    ep,
    ep_t,
    gw_s,
    gw_r,
    gn_t,
    gn_sib,
    gn_s,
    gn_r,
    ge_t,
    ge_sib,
    ge_s,
    ge_r,
    rd_all,
    load_sem,
    enc_ss,
    enc_rs,
    info_ss,
    info_rs,
    epz_ss,
    epz_rs,
    ep_ss,
    ep_rs,
    kv_ss,
    kv_rs,
    ret_ss,
    ret_rs,
    rd_ss,
    rd_rs,
    gn_ss,
    gn_rs,
    ge_ss,
    ge_rs,
    gz_ss,
    gz_rs,
    gy_ss,
    gy_rs,
):
    dp = lax.axis_index("dp")
    mp = lax.axis_index("mp")
    y, z = dp // 4, lax.rem(dp, 4)
    x, c = mp // 2, lax.rem(mp, 2)
    other = 1 - c
    sib = (dp, x * 2 + other)

    def at_x(step):
        return (dp, add4(x, step) * 2 + c)

    def at_y(step):
        return (add4(y, step) * 4 + z, mp)

    def at_z(step):
        return (y * 4 + add4(z, step), mp)

    dp_peers = [(lax.rem(dp + i, 16), mp) for i in range(1, 16)]
    mp_peers = [(dp, lax.rem(mp + i, 8)) for i in range(1, 8)]

    def remote(src, dst, ss, rs, who):
        return pltpu.make_async_remote_copy(
            src_ref=src, dst_ref=dst, send_sem=ss, recv_sem=rs, device_id=who, device_id_type=MESH
        )

    loads = [
        pltpu.make_async_copy(src, dst, load_sem.at[i])
        for i, (src, dst) in enumerate(
            [
                (dec_hbm, dec_v),
                (wq_hbm, wq_v),
                (go_hbm, go_v),
                (wo_hbm, wo_v),
                (wk_hbm, wk_v),
                (wv_hbm, wv_v),
            ]
        )
    ]
    for copy in loads:
        copy.start()

    lane = lax.broadcasted_iota(jnp.int32, (8, 256), 1)
    info_all[mp] = jnp.where(lax.shift_right_logical(lane, 5) == mp, info_ref[...], 0)
    enc_all[mp] = enc_ref[...]

    barrier = pltpu.get_barrier_semaphore()
    for peer in dp_peers + mp_peers:
        pl.semaphore_signal(barrier, inc=1, device_id=peer, device_id_type=MESH)
    pl.semaphore_wait(barrier, 22)

    enc_x = {
        s: remote(enc_ref, enc_all.at[mp], enc_ss.at[s], enc_rs.at[s], at_x(s)) for s in (2, 1, 3)
    }
    for s in (2, 1, 3):
        enc_x[s].start()
    info_c = [
        remote(info_all.at[mp], info_all.at[mp], info_ss.at[i], info_rs.at[i], peer)
        for i, peer in enumerate(mp_peers)
    ]
    for copy in info_c:
        copy.start()

    def enc_forward(s):
        slot = add4(x, 4 - s) * 2 + c
        return remote(enc_all.at[slot], enc_all.at[slot], enc_ss.at[4 + s], enc_rs.at[4 + s], sib)

    enc_f = {s: enc_forward(s) for s in (1, 2, 3)}
    enc_f[0] = remote(enc_ref, enc_all.at[mp], enc_ss.at[4], enc_rs.at[4], sib)
    enc_f[0].start()
    epz = []
    for s in (1, 2, 3):
        for b in range(4):
            column = pl.multiple_of((b * 4 + add4(z, s)) * 256, 256)
            epz.append(
                remote(
                    enc_ref.at[:, pl.ds(column, 256)],
                    ep.at[z, mp, :, pl.ds(b * 256, 256)],
                    epz_ss.at[(s - 1) * 4 + b],
                    epz_rs.at[(s - 1) * 4 + b],
                    at_z(s),
                )
            )
    for copy in epz:
        copy.start()
    for b in range(4):
        column = pl.multiple_of((b * 4 + z) * 256, 256)
        ep[z, mp, :, pl.ds(b * 256, 256)] = enc_ref[:, pl.ds(column, 256)]

    loads[0].wait()

    @pl.loop(0, 8)
    def _(i):
        rows = pl.ds(pl.multiple_of(i * 32, 32), 32)
        wide = dec_v[rows, :].astype(F32)
        rms = jnp.sqrt(jnp.mean(wide * wide, axis=-1, keepdims=True) + 1e-06)
        rms_v[rows, :] = jnp.broadcast_to(rms, (32, 128))
        normed[rows, :] = ((wide / rms) * gain_ref[...].astype(F32)).astype(BF)

    loads[1].wait()
    for h in range(2):
        q_v[h] = dot(normed[...], wq_v[:, h * DH : (h + 1) * DH]).astype(BF)
    for s in (1, 3):
        enc_x[s].wait_recv()
        enc_f[s].start()
    loads[2].wait()
    loads[3].wait()
    for h in range(2):
        gc_v[h] = dot_nt(go_v[...], wo_v[h * DH : (h + 1) * DH, :]).astype(BF)

    for copy in info_c:
        copy.wait_recv()
    info = info_all[0]
    for i in range(1, 8):
        info = info + info_all[i]
    owner = info[0:1, :].astype(F32)
    example = info[1:2, :].astype(F32) + 1.0
    onehot = lax.broadcasted_iota(jnp.int32, (16, 256), 0).astype(F32) == owner
    before = lax.broadcasted_iota(jnp.int32, (256, 256), 0)
    after = lax.broadcasted_iota(jnp.int32, (256, 256), 1)
    same = lax.shift_right_logical(before, 5) == lax.shift_right_logical(after, 5)
    upper = jnp.where(same & (before < after), 1.0, 0.0).astype(BF)
    onehot = jnp.where(onehot, 1.0, 0.0)
    rank = jnp.sum(dot(onehot.astype(BF), upper) * onehot, axis=0, keepdims=True)
    block = lax.shift_right_logical(lax.broadcasted_iota(jnp.int32, (1, 256), 1), 5).astype(F32)
    target = owner * 32.0 + block * 4.0 + rank
    slot_id = lax.broadcasted_iota(jnp.int32, (512, 256), 0).astype(F32)
    placed = jnp.where(slot_id == target, 1.0, 0.0)
    place = placed.astype(BF)
    place_t[...] = placed.T.astype(BF)
    slot_example = jnp.sum(placed * example, axis=1, keepdims=True)
    kv0_s[:, :, 512:640] = jnp.broadcast_to(slot_example, (512, 128)).astype(BF).reshape(16, 32, 128)

    enc_x[2].wait_recv()
    enc_f[2].start()
    for copy in epz:
        copy.wait_recv()
    ep_x = {
        s: remote(ep.at[:, mp], ep.at[:, mp], ep_ss.at[s], ep_rs.at[s], at_x(s)) for s in (2, 1, 3)
    }
    for s in (2, 1, 3):
        ep_x[s].start()

    def ep_forward(s):
        slot = add4(x, 4 - s) * 2 + c
        return remote(ep.at[:, slot], ep.at[:, slot], ep_ss.at[4 + s], ep_rs.at[4 + s], sib)

    ep_f = {s: ep_forward(s) for s in (0, 1, 2, 3)}
    ep_f[0].start()

    for s in range(4):
        enc_f[s].wait_recv()
    loads[4].wait()
    loads[5].wait()
    kv_s, kv_r = [kv0_s, kv1_s], [kv0_r, kv1_r]
    kv_c = []
    for h in range(2):
        rows = enc_all[...].reshape(256, D)
        key = dot(rows, wk_v[:, h * DH : (h + 1) * DH]).astype(BF)
        kv_s[h][:, :, 0:256] = dot(place, key).astype(BF).reshape(16, 32, 256)
        value = dot(rows, wv_v[:, h * DH : (h + 1) * DH]).astype(BF)
        kv_s[h][:, :, 256:512] = dot(place, value).astype(BF).reshape(16, 32, 256)
        copies = [
            remote(kv_s[h].at[peer[0]], kv_r[h].at[dp], kv_ss.at[h, i], kv_rs.at[h, i], peer)
            for i, peer in enumerate(dp_peers)
        ]
        for copy in copies:
            copy.start()
        kv_r[h][dp] = kv_s[h][dp]
        kv_c.append(copies)

    place_of = lax.broadcasted_iota(jnp.int32, (1, 256), 1)
    bound = jnp.int32(0)
    segment = jnp.zeros((1, 256), jnp.int32)
    for e in range(8):
        bound = bound + len_ref[0, e]
        segment = segment + jnp.where(bound <= place_of, 1, 0)
    segment = segment.astype(F32) + 1.0

    for s in (1, 3, 2):
        ep_x[s].wait_recv()
        ep_f[s].start()

    scale = DH**-0.5
    ret_c = []
    row_dot = jnp.zeros((1, 256), F32)
    for h in range(2):
        for copy in kv_c[h]:
            copy.wait_recv()
        if h == 0:
            ex = kv0_r[:, :, 512:640].reshape(512, 128).astype(F32)
            allowed = jnp.concatenate([ex, ex], axis=1) == segment
        key = kv_r[h][:, :, 0:256].reshape(512, 256)
        value = kv_r[h][:, :, 256:512].reshape(512, 256)
        raw = dot_nt(key, q_v[h])
        scores = jnp.where(allowed, raw * scale, -1e30)
        top = jnp.max(scores, axis=0, keepdims=True)
        weights = jnp.where(allowed, jnp.exp(scores - top), 0.0)
        probs = weights / jnp.sum(weights, axis=0, keepdims=True)
        grad_probs = dot_nt(value, gc_v[h])
        inner = jnp.sum(probs * grad_probs, axis=0, keepdims=True)
        grad_scores = (probs * (grad_probs - inner) * scale).astype(BF)
        row_dot = row_dot + jnp.sum(grad_scores.astype(F32) * raw, axis=0, keepdims=True)
        ret_s[h, :, :, 0:256] = dot(grad_scores, q_v[h]).astype(BF).reshape(16, 32, 256)
        ret_s[h, :, :, 256:512] = dot(probs.astype(BF), gc_v[h]).astype(BF).reshape(16, 32, 256)
        copies = [
            remote(ret_s.at[h, peer[0]], ret_r.at[h, dp], ret_ss.at[h, i], ret_rs.at[h, i], peer)
            for i, peer in enumerate(dp_peers)
        ]
        for copy in copies:
            copy.start()
        ret_c.append(copies)
        ret_r[h, dp] = ret_s[h, dp]
        gq_v[:, h * DH : (h + 1) * DH] = dot_tn(grad_scores, key).astype(BF)

    rd_all[mp] = jnp.broadcast_to(row_dot, (8, 256))
    rd_c = [
        remote(rd_all.at[mp], rd_all.at[mp], rd_ss.at[i], rd_rs.at[i], peer)
        for i, peer in enumerate(mp_peers)
    ]
    for copy in rd_c:
        copy.start()

    gz_c = []

    def gather_z(h):
        for copy in ret_c[h]:
            copy.wait_recv()
        own = dot(place_t[...], ret_r[h].reshape(512, 512)).astype(BF)
        g_own[h] = own
        g_all[h, z] = own
        copies = [
            remote(g_own.at[h], g_all.at[h, z], gz_ss.at[h, s - 1], gz_rs.at[h, s - 1], at_z(s))
            for s in (2, 1, 3)
        ]
        for copy in copies:
            copy.start()
        gz_c.append(copies)

    gather_z(0)

    @pl.loop(0, 4)
    def _(i):
        for k in range(2):
            rows = pl.ds(pl.multiple_of((i * 2 + k) * 512, 512), 512)
            gn_t[i, k] = dot_nt(gq_v[...], wq_v[rows, :]).astype(BF)

    gn_pair = remote(gn_t.at[:, other], gn_sib, gn_ss.at[0], gn_rs.at[0], sib)
    gn_pair.start()

    gather_z(1)

    for s in range(4):
        ep_f[s].wait_recv()
    for b in range(4):
        for k in range(4):
            part = ep[k, :, :, b * 256 : (b + 1) * 256].reshape(256, 256)
            ep_t[b, :, k * 256 : (k + 1) * 256] = part.T

    gn_pair.wait_recv()

    @pl.loop(0, 4)
    def _(i):
        gn_s[i] = (gn_t[i, c].astype(F32) + gn_sib[i].astype(F32)).astype(BF)

    gn_x = [
        remote(gn_s.at[add4(x, s)], gn_r.at[s - 1], gn_ss.at[s], gn_rs.at[s], at_x(s))
        for s in (2, 1, 3)
    ]
    for copy in gn_x:
        copy.start()

    @pl.loop(0, 8)
    def _(i):
        rows = pl.ds(pl.multiple_of(i * 512, 512), 512)
        total = jnp.zeros((256, 512), F32)
        for h in range(2):
            total = total + dot_nt(g_own[h, :, 0:256], wk_v[rows, h * DH : (h + 1) * DH])
            total = total + dot_nt(g_own[h, :, 256:512], wv_v[rows, h * DH : (h + 1) * DH])
        total = total.astype(BF).reshape(4, 2, 32, 512)
        for k in range(2):
            ge_t[k, :, :, rows] = total[:, k]

    ge_pair = remote(ge_t.at[other], ge_sib, ge_ss.at[0], ge_rs.at[0], sib)
    ge_pair.start()

    gy_c = []

    def scatter_y(h):
        for copy in gz_c[h]:
            copy.wait_recv()
        every = g_all[h].reshape(1024, 512)
        copies = []
        for s in (2, 1, 3):
            gw_s[h, s - 1] = dot(ep_t[add4(y, s)], every).astype(BF)
            copy = remote(
                gw_s.at[h, s - 1], gw_r.at[h, s - 1], gy_ss.at[h, s - 1], gy_rs.at[h, s - 1], at_y(s)
            )
            copy.start()
            copies.append(copy)
        own = dot(ep_t[y], every)
        gwk_ref[:, h * DH : (h + 1) * DH] = own[:, 0:256]
        gwv_ref[:, h * DH : (h + 1) * DH] = own[:, 256:512]
        gy_c.append(copies)

    scatter_y(0)

    ge_pair.wait_recv()

    @pl.loop(0, 4)
    def _(i):
        ge_s[i] = (ge_t[c, i].astype(F32) + ge_sib[i].astype(F32)).astype(BF)

    ge_x = [
        remote(ge_s.at[add4(x, s)], ge_r.at[s - 1], ge_ss.at[s], ge_rs.at[s], at_x(s))
        for s in (2, 1, 3)
    ]
    for copy in ge_x:
        copy.start()

    scatter_y(1)

    for copy in rd_c:
        copy.wait_recv()
    inner = rd_all[0]
    for i in range(1, 8):
        inner = inner + rd_all[i]
    inner = jnp.broadcast_to(inner[0:1, :], (128, 256)).T * (1.0 / D)
    for copy in gn_x:
        copy.wait_recv()
    share = pl.ds(pl.multiple_of(mp * 512, 512), 512)
    total = gn_s[x].astype(F32)
    for s in range(3):
        total = total + gn_r[s].astype(F32)
    scaled = total * gain_ref[:, share].astype(F32)
    rms = rms_v[:, 0:1]
    unit = dec_v[:, share].astype(F32) / rms
    gd_ref[...] = ((scaled - unit * inner[:, 0:1]) / rms).astype(BF)

    for copy in ge_x:
        copy.wait_recv()
    total = ge_s[x].astype(F32)
    for s in range(3):
        total = total + ge_r[s].astype(F32)
    ge_ref[...] = total.astype(BF)

    for h in range(2):
        columns = slice(h * DH, (h + 1) * DH)
        for copy in gy_c[h]:
            copy.wait_recv()
        total = gw_r[h, 0].astype(F32) + gw_r[h, 1].astype(F32) + gw_r[h, 2].astype(F32)
        gwk_ref[:, columns] = gwk_ref[:, columns] + total[:, 0:256]
        gwv_ref[:, columns] = gwv_ref[:, columns] + total[:, 256:512]

    for copy in (
        list(enc_x.values())
        + list(enc_f.values())
        + info_c
        + epz
        + list(ep_x.values())
        + list(ep_f.values())
        + kv_c[0]
        + kv_c[1]
        + ret_c[0]
        + ret_c[1]
        + rd_c
        + gz_c[0]
        + gz_c[1]
        + [gn_pair, ge_pair]
        + gn_x
        + ge_x
        + gy_c[0]
        + gy_c[1]
    ):
        copy.wait_send()


def local(
    enc,
    enc_owner,
    enc_example,
    dec,
    dec_lengths,
    norm_gain,
    w_query,
    w_key,
    w_value,
    w_out,
    grad_out,
):
    info = jnp.tile(jnp.stack([enc_owner, enc_example]), (4, 8))
    vmem = pl.BlockSpec(memory_space=pltpu.VMEM)
    smem = pl.BlockSpec(memory_space=pltpu.SMEM)
    hbm = pl.BlockSpec(memory_space=pl.ANY)
    dma = pltpu.SemaphoreType.DMA
    V = pltpu.VMEM
    return pl.pallas_call(
        kernel,
        name="cross_attention_grads",
        out_shape=(
            jax.ShapeDtypeStruct((256, 512), BF),
            jax.ShapeDtypeStruct((32, D), BF),
            jax.ShapeDtypeStruct((256, 512), F32),
            jax.ShapeDtypeStruct((256, 512), F32),
        ),
        in_specs=[vmem, vmem, smem, vmem] + [hbm] * 6,
        out_specs=(vmem,) * 4,
        scratch_shapes=[
            V((256, D), BF),
            V((256, D), BF),
            V((D, 512), BF),
            V((D, 512), BF),
            V((D, 512), BF),
            V((512, D), BF),
            V((8, 32, D), BF),
            V((256, D), BF),
            V((256, 128), F32),
            V((8, 8, 256), jnp.int32),
            V((2, 256, 256), BF),
            V((2, 256, 256), BF),
            V((256, 512), BF),
            V((256, 512), BF),
            V((16, 32, 640), BF),
            V((16, 32, 512), BF),
            V((16, 32, 640), BF),
            V((16, 32, 512), BF),
            V((2, 16, 32, 512), BF),
            V((2, 16, 32, 512), BF),
            V((2, 256, 512), BF),
            V((2, 4, 256, 512), BF),
            V((4, 8, 32, 1024), BF),
            V((4, 256, 1024), BF),
            V((2, 3, 256, 512), BF),
            V((2, 3, 256, 512), BF),
            V((4, 2, 256, 512), BF),
            V((4, 256, 512), BF),
            V((4, 256, 512), BF),
            V((3, 256, 512), BF),
            V((2, 4, 32, D), BF),
            V((4, 32, D), BF),
            V((4, 32, D), BF),
            V((3, 32, D), BF),
            V((8, 8, 256), F32),
            dma((6,)),
            dma((8,)),
            dma((8,)),
            dma((7,)),
            dma((7,)),
            dma((12,)),
            dma((12,)),
            dma((8,)),
            dma((8,)),
            dma((2, 15)),
            dma((2, 15)),
            dma((2, 15)),
            dma((2, 15)),
            dma((7,)),
            dma((7,)),
            dma((4,)),
            dma((4,)),
            dma((4,)),
            dma((4,)),
            dma((2, 3)),
            dma((2, 3)),
            dma((2, 3)),
            dma((2, 3)),
        ],
        compiler_params=pltpu.CompilerParams(
            collective_id=0, has_side_effects=True, vmem_limit_bytes=60 * 1024 * 1024
        ),
    )(
        enc,
        info,
        dec_lengths,
        norm_gain.reshape(1, D),
        dec,
        grad_out,
        w_query,
        w_key,
        w_value,
        w_out,
    )


def solution(mesh):
    placed = (
        P(("dp", "mp"), None),
        P(("dp", "mp")),
        P(("dp", "mp")),
        P("dp", None),
        P("dp", None),
        P(),
        P(None, "mp"),
        P(None, "mp"),
        P(None, "mp"),
        P("mp", None),
        P("dp", None),
    )
    return jax.shard_map(
        local,
        mesh=mesh,
        in_specs=placed,
        out_specs=(P("dp", "mp"), P(("dp", "mp"), None), P("dp", "mp"), P("dp", "mp")),
        check_vma=False,
    )
```

```python
import functools

import jax
import jax.numpy as jnp
from jax import lax
from jax.experimental import pallas as pl
from jax.experimental.pallas import tpu as pltpu
from jax.sharding import PartitionSpec as P

MESH = pl.DeviceIdType.MESH
BF = jnp.bfloat16
F32 = jnp.float32
DH = 256
D = 4096
NT = (((1,), (1,)), ((), ()))
TN = (((0,), (0,)), ((), ()))


def dot(a, b):
    return jnp.dot(a, b, preferred_element_type=F32)


def dot_nt(a, b):
    return lax.dot_general(a, b, NT, preferred_element_type=F32)


def dot_tn(a, b):
    return lax.dot_general(a, b, TN, preferred_element_type=F32)


class Copy:
    def __init__(self, copy, started):
        self.copy, self.started, self.received = copy, started, False

    def start(self):
        self.started.append(self)
        self.copy.start()

    def wait_recv(self):
        if not self.received:
            self.received = True
            self.copy.wait_recv()


STOP = 99


def add4(value, step):
    return lax.rem(value + step, 4)


def kernel(
    enc_ref,
    owner_ref,
    example_ref,
    len_ref,
    gain_ref,
    dec_hbm,
    go_hbm,
    wq_hbm,
    wk_hbm,
    wv_hbm,
    wo_hbm,
    gd_hbm,
    ge_hbm,
    gwk_hbm,
    gwv_hbm,
    gd_ref,
    ge_ref,
    gwk_ref,
    gwv_ref,
    dec_v,
    go_v,
    wq_v,
    wk_v,
    wv_v,
    wo_v,
    enc_all,
    normed,
    rms_v,
    info_all,
    q_v,
    gc_v,
    gq_v,
    place_t,
    kv0_s,
    kv1_s,
    kv0_r,
    kv1_r,
    ret_s,
    ret_r,
    g_own,
    g_all,
    ep,
    ep_t,
    gw_s,
    gw_r,
    gn_t,
    gn_sib,
    gn_s,
    gn_r,
    ge_t,
    ge_sib,
    ge_s,
    ge_r,
    rd_all,
    load_sem,
    out_sem,
    enc_ss,
    enc_rs,
    info_ss,
    info_rs,
    epz_ss,
    epz_rs,
    ep_ss,
    ep_rs,
    kv_ss,
    kv_rs,
    ret_ss,
    ret_rs,
    rd_ss,
    rd_rs,
    gn_ss,
    gn_rs,
    ge_ss,
    ge_rs,
    gz_ss,
    gz_rs,
    gy_ss,
    gy_rs,
):
    dp = lax.axis_index("dp")
    mp = lax.axis_index("mp")
    y, z = dp // 4, lax.rem(dp, 4)
    x, c = mp // 2, lax.rem(mp, 2)
    other = 1 - c
    sib = (dp, x * 2 + other)

    def at_x(step):
        return (dp, add4(x, step) * 2 + c)

    def at_y(step):
        return (add4(y, step) * 4 + z, mp)

    def at_z(step):
        return (y * 4 + add4(z, step), mp)

    dp_peers = [(lax.rem(dp + i, 16), mp) for i in range(1, 16)]
    mp_peers = [(dp, lax.rem(mp + i, 8)) for i in range(1, 8)]

    started = []

    def remote(src, dst, ss, rs, who):
        copy = pltpu.make_async_remote_copy(
            src_ref=src, dst_ref=dst, send_sem=ss, recv_sem=rs, device_id=who, device_id_type=MESH
        )
        return Copy(copy, started)

    def finish():
        for i in range(1 if STOP == 0 else 6):
            load(i)
        for copy in started:
            copy.wait_recv()
        for copy in started:
            copy.copy.wait_send()

    loads = [
        pltpu.make_async_copy(src, dst, load_sem.at[i])
        for i, (src, dst) in enumerate(
            [
                (dec_hbm, dec_v),
                (wq_hbm, wq_v),
                (go_hbm, go_v),
                (wo_hbm, wo_v),
                (wk_hbm, wk_v),
                (wv_hbm, wv_v),
            ]
        )
    ]
    loads[0].start()
    loaded = set()

    def load(i):
        if i not in loaded:
            loaded.add(i)
            loads[i].wait()

    lane = lax.broadcasted_iota(jnp.int32, (8, 256), 1)
    line = lax.broadcasted_iota(jnp.int32, (8, 256), 0)
    info = jnp.zeros((8, 256), jnp.int32)
    for r in range(32):
        both = jnp.where(line == 0, owner_ref[r], example_ref[r])
        info = jnp.where(lane == mp * 32 + r, both, info)
    info_all[mp] = info
    enc_all[mp] = enc_ref[...]

    barrier = pltpu.get_barrier_semaphore()
    for peer in dp_peers + mp_peers:
        pl.semaphore_signal(barrier, inc=1, device_id=peer, device_id_type=MESH)
    pl.semaphore_wait(barrier, 22)

    if STOP == 0:
        return finish()
    enc_x = {
        s: remote(enc_ref, enc_all.at[mp], enc_ss.at[s], enc_rs.at[s], at_x(s)) for s in (2, 1, 3)
    }
    for s in (1, 3, 2):
        enc_x[s].start()
    info_c = [
        remote(info_all.at[mp], info_all.at[mp], info_ss.at[i], info_rs.at[i], peer)
        for i, peer in enumerate(mp_peers)
    ]
    for copy in info_c:
        copy.start()

    def enc_forward(s):
        slot = add4(x, 4 - s) * 2 + c
        return remote(enc_all.at[slot], enc_all.at[slot], enc_ss.at[4 + s], enc_rs.at[4 + s], sib)

    enc_f = {s: enc_forward(s) for s in (1, 2, 3)}
    enc_f[0] = remote(enc_ref, enc_all.at[mp], enc_ss.at[4], enc_rs.at[4], sib)
    enc_f[0].start()
    epz = []
    for s in (1, 2, 3):
        for b in range(4):
            column = pl.multiple_of((b * 4 + add4(z, s)) * 256, 256)
            epz.append(
                remote(
                    enc_ref.at[:, pl.ds(column, 256)],
                    ep.at[0, z, mp, :, pl.ds(b * 256, 256)],
                    epz_ss.at[(s - 1) * 4 + b],
                    epz_rs.at[(s - 1) * 4 + b],
                    at_z(s),
                )
            )
        column = pl.multiple_of(add4(y, s) * 1024, 1024)
        epz.append(
            remote(
                enc_ref.at[:, pl.ds(column, 1024)],
                ep.at[1, y, mp],
                epz_ss.at[11 + s],
                epz_rs.at[11 + s],
                at_y(s),
            )
        )
    for copy in epz:
        copy.start()
    for b in range(4):
        column = pl.multiple_of((b * 4 + z) * 256, 256)
        ep[0, z, mp, :, pl.ds(b * 256, 256)] = enc_ref[:, pl.ds(column, 256)]
    ep[1, y, mp] = enc_ref[:, pl.ds(pl.multiple_of(y * 1024, 1024), 1024)]

    for copy in loads[1:]:
        copy.start()

    if STOP == 1:
        return finish()
    load(0)

    @pl.loop(0, 8)
    def _(i):
        rows = pl.ds(pl.multiple_of(i * 32, 32), 32)
        wide = dec_v[rows, :].astype(F32)
        rms = jnp.sqrt(jnp.mean(wide * wide, axis=-1, keepdims=True) + 1e-06)
        rms_v[rows, :] = jnp.broadcast_to(rms, (32, 128))
        normed[rows, :] = ((wide / rms) * gain_ref[...].astype(F32).reshape(1, D)).astype(BF)

    load(1)
    for h in range(2):
        q_v[h] = dot(normed[...], wq_v[:, h * DH : (h + 1) * DH]).astype(BF)
    for s in (1, 3):
        enc_x[s].wait_recv()
        enc_f[s].start()
    if STOP == 2:
        return finish()
    load(2)
    load(3)
    for h in range(2):
        gc_v[h] = dot_nt(go_v[...], wo_v[h * DH : (h + 1) * DH, :]).astype(BF)

    if STOP == 3:
        return finish()
    for copy in info_c:
        copy.wait_recv()
    info = info_all[0]
    for i in range(1, 8):
        info = info + info_all[i]
    owner = info[0:1, :].astype(F32)
    example = info[1:2, :].astype(F32) + 1.0
    onehot = lax.broadcasted_iota(jnp.int32, (16, 256), 0).astype(F32) == owner
    before = lax.broadcasted_iota(jnp.int32, (256, 256), 0)
    after = lax.broadcasted_iota(jnp.int32, (256, 256), 1)
    same = lax.shift_right_logical(before, 5) == lax.shift_right_logical(after, 5)
    upper = jnp.where(same & (before < after), 1.0, 0.0).astype(BF)
    onehot = jnp.where(onehot, 1.0, 0.0)
    rank = jnp.sum(dot(onehot.astype(BF), upper) * onehot, axis=0, keepdims=True)
    block = lax.shift_right_logical(lax.broadcasted_iota(jnp.int32, (1, 256), 1), 5).astype(F32)
    target = owner * 32.0 + block * 4.0 + rank
    slot_id = lax.broadcasted_iota(jnp.int32, (512, 256), 0).astype(F32)
    placed = jnp.where(slot_id == target, 1.0, 0.0)
    place = placed.astype(BF)
    place_t[...] = placed.T.astype(BF)
    slot_example = jnp.sum(placed * example, axis=1, keepdims=True)
    kv0_s[:, :, 512:640] = jnp.broadcast_to(slot_example, (512, 128)).astype(BF).reshape(16, 32, 128)

    if STOP == 4:
        return finish()
    enc_x[2].wait_recv()
    enc_f[2].start()
    for copy in epz:
        copy.wait_recv()
    ep_x = {
        s: remote(ep.at[:, :, mp], ep.at[:, :, mp], ep_ss.at[s], ep_rs.at[s], at_x(s)) for s in (2, 1, 3)
    }
    for s in (2, 1, 3):
        ep_x[s].start()

    def ep_forward(s):
        slot = add4(x, 4 - s) * 2 + c
        return remote(ep.at[:, :, slot], ep.at[:, :, slot], ep_ss.at[4 + s], ep_rs.at[4 + s], sib)

    ep_f = {s: ep_forward(s) for s in (0, 1, 2, 3)}
    ep_f[0].start()

    if STOP == 5:
        return finish()
    for s in range(4):
        enc_f[s].wait_recv()
    load(4)
    load(5)
    kv_s, kv_r = [kv0_s, kv1_s], [kv0_r, kv1_r]
    kv_c = []
    for h in range(2):
        rows = enc_all[...].reshape(256, D)
        key = dot(rows, wk_v[:, h * DH : (h + 1) * DH]).astype(BF)
        kv_s[h][:, :, 0:256] = dot(place, key).astype(BF).reshape(16, 32, 256)
        value = dot(rows, wv_v[:, h * DH : (h + 1) * DH]).astype(BF)
        kv_s[h][:, :, 256:512] = dot(place, value).astype(BF).reshape(16, 32, 256)
        copies = [
            remote(kv_s[h].at[peer[0]], kv_r[h].at[dp], kv_ss.at[h, i], kv_rs.at[h, i], peer)
            for i, peer in enumerate(dp_peers)
        ]
        for copy in copies:
            copy.start()
        kv_r[h][dp] = kv_s[h][dp]
        kv_c.append(copies)

    if STOP == 6:
        return finish()
    place_of = lax.broadcasted_iota(jnp.int32, (1, 256), 1)
    bound = jnp.int32(0)
    segment = jnp.zeros((1, 256), jnp.int32)
    for e in range(8):
        bound = bound + len_ref[0, e]
        segment = segment + jnp.where(bound <= place_of, 1, 0)
    segment = segment.astype(F32) + 1.0

    if STOP == 7:
        return finish()
    scale = DH**-0.5
    ret_c = []
    row_dot = jnp.zeros((1, 256), F32)
    for h in range(2):
        for copy in kv_c[h]:
            copy.wait_recv()
        if h == 0:
            ex = kv0_r[:, :, 512:640].reshape(512, 128).astype(F32)
            allowed = jnp.concatenate([ex, ex], axis=1) == segment
        key = kv_r[h][:, :, 0:256].reshape(512, 256)
        value = kv_r[h][:, :, 256:512].reshape(512, 256)
        raw = dot_nt(key, q_v[h])
        scores = jnp.where(allowed, raw * scale, -1e30)
        top = jnp.max(scores, axis=0, keepdims=True)
        weights = jnp.where(allowed, jnp.exp(scores - top), 0.0)
        probs = weights / jnp.sum(weights, axis=0, keepdims=True)
        grad_probs = dot_nt(value, gc_v[h])
        inner = jnp.sum(probs * grad_probs, axis=0, keepdims=True)
        grad_scores = (probs * (grad_probs - inner) * scale).astype(BF)
        row_dot = row_dot + jnp.sum(grad_scores.astype(F32) * raw, axis=0, keepdims=True)
        ret_s[h, :, :, 0:256] = dot(grad_scores, q_v[h]).astype(BF).reshape(16, 32, 256)
        ret_s[h, :, :, 256:512] = dot(probs.astype(BF), gc_v[h]).astype(BF).reshape(16, 32, 256)
        copies = [
            remote(ret_s.at[h, peer[0]], ret_r.at[h, dp], ret_ss.at[h, i], ret_rs.at[h, i], peer)
            for i, peer in enumerate(dp_peers)
        ]
        for copy in copies:
            copy.start()
        ret_c.append(copies)
        ret_r[h, dp] = ret_s[h, dp]
        gq_v[:, h * DH : (h + 1) * DH] = dot_tn(grad_scores, key).astype(BF)
        for s in [(1, 3), (2,)][h]:
            ep_x[s].wait_recv()
            ep_f[s].start()

    if STOP == 8:
        return finish()
    rd_all[mp] = jnp.broadcast_to(row_dot, (8, 256))
    rd_c = [
        remote(rd_all.at[mp], rd_all.at[mp], rd_ss.at[i], rd_rs.at[i], peer)
        for i, peer in enumerate(mp_peers)
    ]
    for copy in rd_c:
        copy.start()

    gz_c = []
    gather_at, reduce_at = [at_z, at_y], [at_y, at_z]
    gather_me, reduce_me = [z, y], [y, z]

    def gather(h):
        here = gather_me[h]
        for copy in ret_c[h]:
            copy.wait_recv()
        own = dot(place_t[...], ret_r[h].reshape(512, 512)).astype(BF)
        g_own[h] = own
        g_all[h, here] = own
        copies = [
            remote(
                g_own.at[h], g_all.at[h, here], gz_ss.at[h, s - 1], gz_rs.at[h, s - 1], gather_at[h](s)
            )
            for s in (2, 1, 3)
        ]
        for copy in copies:
            copy.start()
        gz_c.append(copies)

    gather(0)

    if STOP == 9:
        return finish()
    @pl.loop(0, 4)
    def _(i):
        for k in range(2):
            rows = pl.ds(pl.multiple_of((i * 2 + k) * 512, 512), 512)
            gn_t[i, k] = dot_nt(gq_v[...], wq_v[rows, :]).astype(BF)

    gn_pair = remote(gn_t.at[:, other], gn_sib, gn_ss.at[0], gn_rs.at[0], sib)
    gn_pair.start()

    gather(1)

    if STOP == 10:
        return finish()
    for s in range(4):
        ep_f[s].wait_recv()
    for h in range(2):
        for b in range(4):
            for k in range(4):
                part = ep[h, k, :, :, b * 256 : (b + 1) * 256].reshape(256, 256)
                ep_t[h, b, :, k * 256 : (k + 1) * 256] = part.T

    gn_pair.wait_recv()

    @pl.loop(0, 4)
    def _(i):
        gn_s[i] = (gn_t[i, c].astype(F32) + gn_sib[i].astype(F32)).astype(BF)

    gn_x = [
        remote(gn_s.at[add4(x, s)], gn_r.at[s - 1], gn_ss.at[s], gn_rs.at[s], at_x(s))
        for s in (2, 1, 3)
    ]
    for copy in gn_x:
        copy.start()

    if STOP == 11:
        return finish()
    @pl.loop(0, 8)
    def _(i):
        rows = pl.ds(pl.multiple_of(i * 512, 512), 512)
        total = jnp.zeros((256, 512), F32)
        for h in range(2):
            total = total + dot_nt(g_own[h, :, 0:256], wk_v[rows, h * DH : (h + 1) * DH])
            total = total + dot_nt(g_own[h, :, 256:512], wv_v[rows, h * DH : (h + 1) * DH])
        total = total.astype(BF).reshape(4, 2, 32, 512)
        for k in range(2):
            ge_t[k, :, :, rows] = total[:, k]

    ge_pair = remote(ge_t.at[other], ge_sib, ge_ss.at[0], ge_rs.at[0], sib)
    ge_pair.start()

    if STOP == 12:
        return finish()
    gy_c = []

    def scatter(h):
        for copy in gz_c[h]:
            copy.wait_recv()
        every = g_all[h].reshape(1024, 512)
        here = reduce_me[h]
        copies = []
        for s in (2, 1, 3):
            gw_s[h, s - 1] = dot(ep_t[h, add4(here, s)], every).astype(BF)
            copy = remote(
                gw_s.at[h, s - 1],
                gw_r.at[h, s - 1],
                gy_ss.at[h, s - 1],
                gy_rs.at[h, s - 1],
                reduce_at[h](s),
            )
            copy.start()
            copies.append(copy)
        own = dot(ep_t[h, here], every)
        gwk_ref[:, h * DH : (h + 1) * DH] = own[:, 0:256]
        gwv_ref[:, h * DH : (h + 1) * DH] = own[:, 256:512]
        gy_c.append(copies)

    scatter(0)

    ge_pair.wait_recv()

    @pl.loop(0, 4)
    def _(i):
        ge_s[i] = (ge_t[c, i].astype(F32) + ge_sib[i].astype(F32)).astype(BF)

    ge_x = [
        remote(ge_s.at[add4(x, s)], ge_r.at[s - 1], ge_ss.at[s], ge_rs.at[s], at_x(s))
        for s in (2, 1, 3)
    ]
    for copy in ge_x:
        copy.start()

    if STOP == 13:
        return finish()
    scatter(1)

    if STOP == 14:
        return finish()
    outs = [
        pltpu.make_async_copy(src, dst, out_sem.at[i])
        for i, (src, dst) in enumerate(
            [(gd_ref, gd_hbm), (ge_ref, ge_hbm), (gwk_ref, gwk_hbm), (gwv_ref, gwv_hbm)]
        )
    ]

    for copy in rd_c:
        copy.wait_recv()
    inner = rd_all[0]
    for i in range(1, 8):
        inner = inner + rd_all[i]
    inner = jnp.broadcast_to(inner[0:1, :], (128, 256)).T * (1.0 / D)
    for copy in gn_x:
        copy.wait_recv()
    share = pl.ds(pl.multiple_of(mp * 512, 512), 512)
    total = gn_s[x].astype(F32)
    for s in range(3):
        total = total + gn_r[s].astype(F32)
    scaled = total * gain_ref[share].astype(F32).reshape(1, 512)
    rms = rms_v[:, 0:1]
    unit = dec_v[:, share].astype(F32) / rms
    gd_ref[...] = ((scaled - unit * inner[:, 0:1]) / rms).astype(BF)
    outs[0].start()

    for copy in ge_x:
        copy.wait_recv()
    total = ge_s[x].astype(F32)
    for s in range(3):
        total = total + ge_r[s].astype(F32)
    ge_ref[...] = total.astype(BF)
    outs[1].start()

    for h in range(2):
        columns = slice(h * DH, (h + 1) * DH)
        for copy in gy_c[h]:
            copy.wait_recv()
        total = gw_r[h, 0].astype(F32) + gw_r[h, 1].astype(F32) + gw_r[h, 2].astype(F32)
        gwk_ref[:, columns] = gwk_ref[:, columns] + total[:, 0:256]
        gwv_ref[:, columns] = gwv_ref[:, columns] + total[:, 256:512]

    outs[2].start()
    outs[3].start()
    finish()
    for copy in outs:
        copy.wait()


def hand_on(a, b, c, d, a_out, b_out, c_out, d_out):
    a_out[...] = a[...]
    b_out[...] = b[...]
    c_out[...] = c[...]
    d_out[...] = d[...]


def local(
    enc,
    enc_owner,
    enc_example,
    dec,
    dec_lengths,
    norm_gain,
    w_query,
    w_key,
    w_value,
    w_out,
    grad_out,
):
    vmem = pl.BlockSpec(memory_space=pltpu.VMEM)
    smem = pl.BlockSpec(memory_space=pltpu.SMEM)
    hbm = pl.BlockSpec(memory_space=pl.ANY)
    dma = pltpu.SemaphoreType.DMA
    V = pltpu.VMEM
    shapes = (
        jax.ShapeDtypeStruct((256, 512), BF),
        jax.ShapeDtypeStruct((32, D), BF),
        jax.ShapeDtypeStruct((256, 512), F32),
        jax.ShapeDtypeStruct((256, 512), F32),
    )
    results = pl.pallas_call(
        kernel,
        name="cross_attention_grads",
        out_shape=shapes,
        in_specs=[vmem, smem, smem, smem, vmem] + [hbm] * 6,
        out_specs=(hbm,) * 4,
        scratch_shapes=[
            V((256, 512), BF),
            V((32, D), BF),
            V((256, 512), F32),
            V((256, 512), F32),
            V((256, D), BF),
            V((256, D), BF),
            V((D, 512), BF),
            V((D, 512), BF),
            V((D, 512), BF),
            V((512, D), BF),
            V((8, 32, D), BF),
            V((256, D), BF),
            V((256, 128), F32),
            V((8, 8, 256), jnp.int32),
            V((2, 256, 256), BF),
            V((2, 256, 256), BF),
            V((256, 512), BF),
            V((256, 512), BF),
            V((16, 32, 640), BF),
            V((16, 32, 512), BF),
            V((16, 32, 640), BF),
            V((16, 32, 512), BF),
            V((2, 16, 32, 512), BF),
            V((2, 16, 32, 512), BF),
            V((2, 256, 512), BF),
            V((2, 4, 256, 512), BF),
            V((2, 4, 8, 32, 1024), BF),
            V((2, 4, 256, 1024), BF),
            V((2, 3, 256, 512), BF),
            V((2, 3, 256, 512), BF),
            V((4, 2, 256, 512), BF),
            V((4, 256, 512), BF),
            V((4, 256, 512), BF),
            V((3, 256, 512), BF),
            V((2, 4, 32, D), BF),
            V((4, 32, D), BF),
            V((4, 32, D), BF),
            V((3, 32, D), BF),
            V((8, 8, 256), F32),
            dma((6,)),
            dma((4,)),
            dma((8,)),
            dma((8,)),
            dma((7,)),
            dma((7,)),
            dma((15,)),
            dma((15,)),
            dma((8,)),
            dma((8,)),
            dma((2, 15)),
            dma((2, 15)),
            dma((2, 15)),
            dma((2, 15)),
            dma((7,)),
            dma((7,)),
            dma((4,)),
            dma((4,)),
            dma((4,)),
            dma((4,)),
            dma((2, 3)),
            dma((2, 3)),
            dma((2, 3)),
            dma((2, 3)),
        ],
        compiler_params=pltpu.CompilerParams(
            collective_id=0, has_side_effects=True, vmem_limit_bytes=60 * 1024 * 1024
        ),
    )(
        enc,
        enc_owner,
        enc_example,
        dec_lengths,
        norm_gain,
        dec,
        grad_out,
        w_query,
        w_key,
        w_value,
        w_out,
    )
    return pl.pallas_call(
        hand_on,
        name="hand_on",
        out_shape=shapes,
        in_specs=[vmem] * 4,
        out_specs=(vmem,) * 4,
    )(*results)


def solution(mesh):
    placed = (
        P(("dp", "mp"), None),
        P(("dp", "mp")),
        P(("dp", "mp")),
        P("dp", None),
        P("dp", None),
        P(),
        P(None, "mp"),
        P(None, "mp"),
        P(None, "mp"),
        P("mp", None),
        P("dp", None),
    )
    return jax.shard_map(
        local,
        mesh=mesh,
        in_specs=placed,
        out_specs=(P("dp", "mp"), P(("dp", "mp"), None), P("dp", "mp"), P("dp", "mp")),
        check_vma=False,
    )
```

```python
import functools

import jax
import jax.numpy as jnp
from jax import lax
from jax.experimental import pallas as pl
from jax.experimental.pallas import tpu as pltpu
from jax.sharding import PartitionSpec as P

MESH = pl.DeviceIdType.MESH
BF = jnp.bfloat16
F32 = jnp.float32
DH = 256
D = 4096
NT = (((1,), (1,)), ((), ()))
TN = (((0,), (0,)), ((), ()))


def dot(a, b):
    return jnp.dot(a, b, preferred_element_type=F32)


def dot_nt(a, b):
    return lax.dot_general(a, b, NT, preferred_element_type=F32)


def dot_tn(a, b):
    return lax.dot_general(a, b, TN, preferred_element_type=F32)


class Copy:
    def __init__(self, copy, started):
        self.copy, self.started, self.received = copy, started, False

    def start(self):
        self.started.append(self)
        self.copy.start()

    def wait_recv(self):
        if not self.received:
            self.received = True
            self.copy.wait_recv()


def add4(value, step):
    return lax.rem(value + step, 4)


def kernel(
    enc_ref,
    owner_ref,
    example_ref,
    len_ref,
    gain_ref,
    dec_hbm,
    go_hbm,
    wq_hbm,
    wk_hbm,
    wv_hbm,
    wo_hbm,
    gd_hbm,
    ge_hbm,
    gwk_hbm,
    gwv_hbm,
    gd_ref,
    ge_ref,
    gwk_ref,
    gwv_ref,
    dec_v,
    go_v,
    wq_v,
    wk_v,
    wv_v,
    wo_v,
    enc_all,
    normed,
    rms_v,
    info_all,
    q_v,
    gc_v,
    gq_v,
    perm_v,
    place_t,
    one_s,
    one_b,
    one_r,
    ex_s,
    ex_r,
    kv_s,
    kv_r,
    key_v,
    value_v,
    ret_s,
    ret_r,
    g_own,
    g_all,
    ep,
    ep_t,
    gw_s,
    gw_r,
    gw_q,
    gn_t,
    gn_sib,
    gn_s,
    gn_r,
    gn_q,
    ge_t,
    ge_sib,
    ge_s,
    ge_r,
    ge_q,
    back_s,
    back_r,
    rd_all,
    load_sem,
    out_sem,
    one_ss,
    one_rs,
    enc_ss,
    enc_rs,
    eno_ss,
    eno_rs,
    ex_ss,
    ex_rs,
    info_ss,
    info_rs,
    epz_ss,
    epz_rs,
    ep_ss,
    ep_rs,
    kv_ss,
    kv_rs,
    ret_ss,
    ret_rs,
    rd_ss,
    rd_rs,
    gn_ss,
    gn_rs,
    ge_ss,
    ge_rs,
    gz_ss,
    gz_rs,
    gy_ss,
    gy_rs,
    back_ss,
    back_rs,
):
    dp = lax.axis_index("dp")
    mp = lax.axis_index("mp")
    y, z = dp // 4, lax.rem(dp, 4)
    x, c = mp // 2, lax.rem(mp, 2)
    other = 1 - c
    sib = (dp, x * 2 + other)

    def at_x(step):
        return (dp, add4(x, step) * 2 + c)

    def at_y(step):
        return (add4(y, step) * 4 + z, mp)

    def at_z(step):
        return (y * 4 + add4(z, step), mp)

    dp_peers = [(lax.rem(dp + i, 16), mp) for i in range(1, 16)]
    mp_peers = [(dp, lax.rem(mp + i, 8)) for i in range(1, 8)]

    started = []

    def remote(src, dst, ss, rs, who):
        copy = pltpu.make_async_remote_copy(
            src_ref=src, dst_ref=dst, send_sem=ss, recv_sem=rs, device_id=who, device_id_type=MESH
        )
        return Copy(copy, started)

    def finish():
        for i in range(6):
            load(i)
        for copy in started:
            copy.wait_recv()
        for copy in started:
            copy.copy.wait_send()

    class Gather:
        def __init__(self, src, slot, halves, place, at, ss, rs):
            self.slot, self.halves, self.place, self.at, self.ss, self.rs = slot, halves, place, at, ss, rs
            self.one = [remote(src, slot(place), ss.at[i], rs.at[i], at(s)) for i, s in enumerate((1, 3))]
            for copy in self.one:
                copy.start()

        def relay(self):
            self.two = []
            for i, s in enumerate((1, 3)):
                self.one[i].wait_recv()
                half = self.halves(self.slot(add4(self.place, 4 - s)))[i]
                copy = remote(half, half, self.ss.at[2 + i], self.rs.at[2 + i], self.at(s))
                copy.start()
                self.two.append(copy)

        def wait(self):
            for copy in self.two:
                copy.wait_recv()

    class Reduce:
        def __init__(self, term, halves, far, got, at, ss, rs):
            self.term, self.halves, self.far, self.got = term, halves, far, got
            self.at, self.ss, self.rs = at, ss, rs
            self.copies = []

        def send(self, src, dst, i, s):
            copy = remote(src, dst, self.ss.at[i], self.rs.at[i], self.at(s))
            copy.start()
            self.copies.append(copy)

        def send_far(self):
            for i, s in enumerate((1, 3)):
                self.send(self.halves(self.term(2))[i], self.far.at[i], i, s)

        def send_near(self):
            for i, s in enumerate((1, 3)):
                self.send(self.halves(self.term(s))[1 - i], self.halves(self.got.at[i])[1 - i], 2 + i, s)

        def relay(self):
            for i, s in enumerate((1, 3)):
                self.copies[i].wait_recv()
                half = self.halves(self.term(s))[i]
                half[...] = (half[...].astype(F32) + self.far[i].astype(F32)).astype(BF)
                self.send(half, self.halves(self.got.at[i])[i], 4 + i, s)

        def total(self, own):
            for copy in self.copies:
                copy.wait_recv()
            return own + self.got[0].astype(F32) + self.got[1].astype(F32)

    loads = [
        pltpu.make_async_copy(src, dst, load_sem.at[i])
        for i, (src, dst) in enumerate(
            [
                (dec_hbm, dec_v),
                (wq_hbm, wq_v),
                (go_hbm, go_v),
                (wo_hbm, wo_v),
                (wk_hbm, wk_v),
                (wv_hbm, wv_v),
            ]
        )
    ]
    loads[0].start()
    loaded = set()

    def load(i):
        if i not in loaded:
            loaded.add(i)
            loads[i].wait()

    barrier = pltpu.get_barrier_semaphore()
    for peer in dp_peers + mp_peers:
        pl.semaphore_signal(barrier, inc=1, device_id=peer, device_id_type=MESH)

    line = lax.broadcasted_iota(jnp.int32, (8, 128), 0)
    lane = lax.broadcasted_iota(jnp.int32, (8, 128), 1)
    ids = jnp.full((8, 128), -1, jnp.int32)
    for r in range(32):
        ids = jnp.where(lane == r, jnp.where(line == 0, owner_ref[r], example_ref[r]), ids)
    ids = ids.astype(F32)
    owner = ids[0:1, :]
    example = ids[1:2, :] + 1.0
    before = lax.broadcasted_iota(jnp.int32, (128, 128), 0)
    after = lax.broadcasted_iota(jnp.int32, (128, 128), 1)
    upper = jnp.where(before < after, 1.0, 0.0).astype(BF)
    onehot = lax.broadcasted_iota(jnp.int32, (16, 128), 0).astype(F32) == owner
    onehot = jnp.where(onehot, 1.0, 0.0)
    rank = jnp.sum(dot(onehot.astype(BF), upper) * onehot, axis=0, keepdims=True)
    later = jnp.where(rank > 0.5, 1.0, 0.0)
    order = dot(jnp.broadcast_to(later, (16, 128)).astype(BF), upper)[0:1, :]
    position = jnp.where(rank > 0.5, 16.0 + order, owner)
    perm = lax.broadcasted_iota(jnp.int32, (32, 128), 0).astype(F32) == position
    perm = jnp.where(perm, 1.0, 0.0)
    perm_v[...] = perm
    perm = perm[:, 0:32].astype(BF)
    lane_of = jnp.where(rank > 0.5, order + (mp * 16).astype(F32), -1.0)
    moved = jnp.broadcast_to(lane_of, (128, 128)).T == after.astype(F32)
    moved = jnp.where(moved, 1.0, 0.0).astype(BF)
    facts = jnp.where(line == 0, owner, jnp.where(line == 1, rank, example))
    facts = jnp.concatenate([facts, facts], axis=0).astype(BF)
    info_all[mp] = dot(facts, moved)[0:8, :]
    first = jnp.sum(perm_v[0:16, :] * example, axis=1, keepdims=True)
    for i in range(8):
        columns = slice(i * 512, (i + 1) * 512)
        rows = dot(perm, enc_ref[:, columns])
        enc_all[mp, 16:32, columns] = rows[16:32, :].astype(BF)
        one_s[:, i * 4 : (i + 1) * 4, :] = rows[0:16, :].reshape(16, 4, 128)
    one_s[:, 32:48, :] = jnp.broadcast_to(first.reshape(16, 1, 1), (16, 16, 128))
    one_b[...] = one_s[...].astype(BF)

    pl.semaphore_wait(barrier, 22)

    def later_halves(block):
        return block.at[:, 0 : D // 2], block.at[:, D // 2 : D]

    mine = enc_all.at[mp, 16:32, 0:D]
    later_g = Gather(
        mine, lambda place: enc_all.at[place * 2 + c, 16:32, 0:D], later_halves, x, at_x, enc_ss, enc_rs
    )
    one_c = [
        remote(one_b.at[peer[0]], one_r.at[dp], one_ss.at[i], one_rs.at[i], peer)
        for i, peer in enumerate(dp_peers)
    ]
    for copy in one_c:
        copy.start()
    one_r[dp] = one_b[dp]
    info_c = [
        remote(info_all.at[mp], info_all.at[mp], info_ss.at[i], info_rs.at[i], peer)
        for i, peer in enumerate(mp_peers)
    ]
    for copy in info_c:
        copy.start()

    def enc_forward(s):
        block = enc_all.at[add4(x, 4 - s) * 2 + c, 16:32, 0:D]
        return remote(block, block, enc_ss.at[4 + s], enc_rs.at[4 + s], sib)

    enc_f = {s: enc_forward(s) for s in range(4)}
    enc_f[0].start()

    for copy in loads[1:]:
        copy.start()

    load(0)

    @pl.loop(0, 8)
    def _(i):
        rows = pl.ds(pl.multiple_of(i * 32, 32), 32)
        wide = dec_v[rows, :].astype(F32)
        rms = jnp.sqrt(jnp.mean(wide * wide, axis=-1, keepdims=True) + 1e-06)
        rms_v[rows, :] = jnp.broadcast_to(rms, (32, 128))
        normed[rows, :] = ((wide * (1.0 / rms)) * gain_ref[...].astype(F32).reshape(1, D)).astype(BF)

    later_g.relay()
    for s in (1, 3):
        enc_f[s].start()
    for copy in one_c:
        copy.wait_recv()
    rows = one_r[...].astype(F32)
    enc_all[mp, 0:16, 0:D] = rows[:, 0:32, :].reshape(16, D).astype(BF)
    enc_all[mp, 0:16, D : D + 128] = rows[:, 32, :].astype(BF)
    def first_halves(block):
        return block.at[:, 0 : D // 2], block.at[:, D // 2 : D + 128]

    first_g = Gather(
        enc_all.at[mp, 0:16, :],
        lambda place: enc_all.at[place * 2 + c, 0:16, :],
        first_halves,
        x,
        at_x,
        eno_ss,
        eno_rs,
    )

    def eno_forward(s):
        block = enc_all.at[add4(x, 4 - s) * 2 + c, 0:16, :]
        return remote(block, block, eno_ss.at[4 + s], eno_rs.at[4 + s], sib)

    eno_f = {s: eno_forward(s) for s in range(4)}
    eno_f[0].start()
    epz = []
    for s in (1, 2, 3):
        for b in range(4):
            column = pl.multiple_of((b * 4 + add4(z, s)) * 256, 256)
            epz.append(
                remote(
                    enc_all.at[mp, :, pl.ds(column, 256)],
                    ep.at[0, z, mp, :, pl.ds(b * 256, 256)],
                    epz_ss.at[(s - 1) * 4 + b],
                    epz_rs.at[(s - 1) * 4 + b],
                    at_z(s),
                )
            )
        column = pl.multiple_of(add4(y, s) * 1024, 1024)
        epz.append(
            remote(
                enc_all.at[mp, :, pl.ds(column, 1024)],
                ep.at[1, y, mp],
                epz_ss.at[11 + s],
                epz_rs.at[11 + s],
                at_y(s),
            )
        )
    for copy in epz:
        copy.start()
    for b in range(4):
        column = pl.multiple_of((b * 4 + z) * 256, 256)
        ep[0, z, mp, :, pl.ds(b * 256, 256)] = enc_all[mp, :, pl.ds(column, 256)]
    ep[1, y, mp] = enc_all[mp, :, pl.ds(pl.multiple_of(y * 1024, 1024), 1024)]

    load(1)
    for h in range(2):
        q_v[h] = dot(normed[...], wq_v[:, h * DH : (h + 1) * DH]).astype(BF)
    def gc_and_first():
        load(2)
        load(3)
        for h in range(2):
            gc_v[h] = dot_nt(go_v[...], wo_v[h * DH : (h + 1) * DH, :]).astype(BF)
        for s in range(4):
            eno_f[s].wait_recv()
        rows = enc_all[:, 0:16, 0:D].reshape(128, D)
        for h in range(2):
            columns = slice(h * DH, (h + 1) * DH)
            key_v[h, 0:128, :] = dot(rows, wk_v[:, columns]).astype(BF)
            value_v[h, 0:128, :] = dot(rows, wv_v[:, columns]).astype(BF)

    first_g.relay()
    for s in (1, 3):
        eno_f[s].start()

    for copy in info_c:
        copy.wait_recv()
    info = info_all[0]
    for i in range(1, 8):
        info = info + info_all[i]
    block = lax.shift_right_logical(lax.broadcasted_iota(jnp.int32, (1, 128), 1), 4).astype(F32)
    target = info[0:1, :] * 24.0 + block * 3.0 + info[1:2, :] - 1.0
    slot_id = lax.broadcasted_iota(jnp.int32, (384, 128), 0).astype(F32)
    placed = jnp.where(slot_id == target, 1.0, 0.0)
    place = placed.astype(BF)
    place_t[...] = placed.T.astype(BF)
    slot_example = jnp.sum(placed * info[2:3, :], axis=1, keepdims=True)
    slot_example = jnp.broadcast_to(slot_example, (384, 128)).reshape(16, 24, 128)
    ex_s[...] = jnp.concatenate([slot_example, jnp.zeros((16, 8, 128), F32)], axis=1).astype(BF)
    ex_c = [
        remote(ex_s.at[peer[0]], ex_r.at[dp], ex_ss.at[i], ex_rs.at[i], peer)
        for i, peer in enumerate(dp_peers)
    ]
    for copy in ex_c:
        copy.start()
    ex_r[dp] = ex_s[dp]

    later_g.wait()
    enc_f[2].start()
    for s in range(4):
        enc_f[s].wait_recv()
    load(4)
    load(5)
    kv_c = []
    for h in range(2):
        columns = slice(h * DH, (h + 1) * DH)
        rows = enc_all[:, 16:32, 0:D].reshape(128, D)
        key = dot(place, dot(rows, wk_v[:, columns]).astype(BF)).reshape(16, 24, 256)
        value = dot(place, dot(rows, wv_v[:, columns]).astype(BF)).reshape(16, 24, 256)
        kv_s[h] = jnp.concatenate([key, value], axis=1).astype(BF)
        copies = [
            remote(kv_s.at[h, peer[0]], kv_r.at[h, dp], kv_ss.at[h, i], kv_rs.at[h, i], peer)
            for i, peer in enumerate(dp_peers)
        ]
        for copy in copies:
            copy.start()
        kv_r[h, dp] = kv_s[h, dp]
        kv_c.append(copies)

    first_g.wait()
    eno_f[2].start()
    for copy in epz:
        copy.wait_recv()
    ep_g = Gather(
        ep.at[:, :, mp],
        lambda place: ep.at[:, :, place * 2 + c],
        lambda block: (block.at[0], block.at[1]),
        x,
        at_x,
        ep_ss,
        ep_rs,
    )

    def ep_forward(s):
        block = ep.at[:, :, add4(x, 4 - s) * 2 + c]
        return remote(block, block, ep_ss.at[4 + s], ep_rs.at[4 + s], sib)

    ep_f = {s: ep_forward(s) for s in range(4)}
    ep_f[0].start()

    gc_and_first()

    place_of = lax.broadcasted_iota(jnp.int32, (1, 256), 1)
    bound = jnp.int32(0)
    segment = jnp.zeros((1, 256), jnp.int32)
    for e in range(8):
        bound = bound + len_ref[0, e]
        segment = segment + jnp.where(bound <= place_of, 1, 0)
    segment = segment.astype(F32) + 1.0

    scale = DH**-0.5
    ret_c = []
    gz_g = [[], []]
    gather_at, reduce_at = [at_z, at_y], [at_y, at_z]
    gather_me, reduce_me = [z, y], [y, z]

    def gather(h, part):
        here = gather_me[h]
        g_all[h, here, :, part] = g_own[h, :, part]
        gz_g[h].append(
            Gather(
                g_own.at[h, :, part],
                lambda place: g_all.at[h, place, :, part],
                lambda block: (block.at[0:4], block.at[4:8]),
                here,
                gather_at[h],
                gz_ss.at[h, part],
                gz_rs.at[h, part],
            )
        )

    row_dot = jnp.zeros((1, 256), F32)
    for copy in ex_c:
        copy.wait_recv()
    ex = enc_all[:, 0:16, D : D + 128].reshape(128, 128).astype(F32)
    ex = jnp.concatenate([ex, ex_r[...].astype(F32)[:, 0:24, :].reshape(384, 128)], axis=0)
    allowed = jnp.concatenate([ex, ex], axis=1) == segment
    for h in range(2):
        for copy in kv_c[h]:
            copy.wait_recv()
        both = kv_r[h].astype(F32)
        key_v[h, 128:512, :] = both[:, 0:24, :].reshape(384, 256).astype(BF)
        value_v[h, 128:512, :] = both[:, 24:48, :].reshape(384, 256).astype(BF)
        key = key_v[h]
        value = value_v[h]
        raw = dot_nt(key, q_v[h])
        scores = jnp.where(allowed, raw * scale, -1e30)
        top = jnp.max(scores, axis=0, keepdims=True)
        weights = jnp.where(allowed, jnp.exp(scores - top), 0.0)
        probs = weights / jnp.sum(weights, axis=0, keepdims=True)
        grad_probs = dot_nt(value, gc_v[h])
        inner = jnp.sum(probs * grad_probs, axis=0, keepdims=True)
        grad_scores = (probs * (grad_probs - inner) * scale).astype(BF)
        row_dot = row_dot + jnp.sum(grad_scores.astype(F32) * raw, axis=0, keepdims=True)
        grad_key = dot(grad_scores, q_v[h])
        grad_value = dot(probs.astype(BF), gc_v[h])
        ret_s[h] = jnp.concatenate(
            [grad_key[128:512, :].reshape(16, 24, 256), grad_value[128:512, :].reshape(16, 24, 256)],
            axis=1,
        ).astype(BF)
        copies = [
            remote(ret_s.at[h, peer[0]], ret_r.at[h, dp], ret_ss.at[h, i], ret_rs.at[h, i], peer)
            for i, peer in enumerate(dp_peers)
        ]
        for copy in copies:
            copy.start()
        ret_c.append(copies)
        ret_r[h, dp] = ret_s[h, dp]
        g_own[h, :, 0, :, 0:256] = grad_key[0:128, :].astype(BF).reshape(8, 16, 256)
        g_own[h, :, 0, :, 256:512] = grad_value[0:128, :].astype(BF).reshape(8, 16, 256)
        gather(h, 0)
        gq_v[:, h * DH : (h + 1) * DH] = dot_tn(grad_scores, key).astype(BF)

    rd_all[mp] = jnp.broadcast_to(row_dot, (8, 256))
    rd_c = [
        remote(rd_all.at[mp], rd_all.at[mp], rd_ss.at[i], rd_rs.at[i], peer)
        for i, peer in enumerate(mp_peers)
    ]
    for copy in rd_c:
        copy.start()

    def take_back(h):
        for copy in ret_c[h]:
            copy.wait_recv()
        both = ret_r[h].astype(F32)
        for k in range(2):
            back = both[:, k * 24 : (k + 1) * 24, :].reshape(384, 256).astype(BF)
            back = dot(place_t[...], back).astype(BF).reshape(8, 16, 256)
            g_own[h, :, 1, :, k * 256 : (k + 1) * 256] = back
        gather(h, 1)

    @pl.loop(0, 4)
    def _(i):
        for k in range(2):
            rows = pl.ds(pl.multiple_of((i * 2 + k) * 512, 512), 512)
            gn_t[i, k] = dot_nt(gq_v[...], wq_v[rows, :]).astype(BF)

    gn_pair = remote(gn_t.at[:, other], gn_sib, gn_ss.at[6], gn_rs.at[6], sib)
    gn_pair.start()

    ep_g.relay()
    for s in (1, 3):
        ep_f[s].start()
    for h in range(2):
        gz_g[h][0].relay()
    take_back(0)
    take_back(1)

    gn_pair.wait_recv()

    @pl.loop(0, 4)
    def _(i):
        gn_s[i] = (gn_t[i, c].astype(F32) + gn_sib[i].astype(F32)).astype(BF)

    def row_halves(block):
        return block.at[0:128], block.at[128:256]

    gn_red = Reduce(lambda s: gn_s.at[add4(x, s)], row_halves, gn_q, gn_r, at_x, gn_ss, gn_rs)
    gn_red.send_far()
    gn_red.send_near()

    @pl.loop(0, 8)
    def _(i):
        rows = pl.ds(pl.multiple_of(i * 512, 512), 512)
        total = jnp.zeros((256, 512), F32)
        for h in range(2):
            rows_h = g_own[h].reshape(256, 512)
            total = total + dot_nt(rows_h[:, 0:256], wk_v[rows, h * DH : (h + 1) * DH])
            total = total + dot_nt(rows_h[:, 256:512], wv_v[rows, h * DH : (h + 1) * DH])
        total = total.astype(BF).reshape(4, 2, 32, 512)
        for k in range(2):
            ge_t[k, :, :, rows] = total[:, k]

    ge_pair = remote(ge_t.at[other], ge_sib, ge_ss.at[6], ge_rs.at[6], sib)
    ge_pair.start()

    for h in range(2):
        gz_g[h][1].relay()

    ep_g.wait()
    ep_f[2].start()
    for s in range(4):
        ep_f[s].wait_recv()
    for h in range(2):
        for b in range(4):
            for k in range(4):
                part = ep[h, k, :, :, b * 256 : (b + 1) * 256].reshape(256, 256)
                ep_t[h, b, :, k * 256 : (k + 1) * 256] = part.T

    ge_pair.wait_recv()

    @pl.loop(0, 4)
    def _(i):
        ge_s[i] = (ge_t[c, i].astype(F32) + ge_sib[i].astype(F32)).astype(BF)

    ge_red = Reduce(
        lambda s: ge_s.at[add4(x, s)],
        lambda block: (block.at[0:16], block.at[16:32]),
        ge_q,
        ge_r,
        at_x,
        ge_ss,
        ge_rs,
    )
    ge_red.send_far()
    ge_red.send_near()
    gn_red.relay()

    gy_red = []

    def scatter(h):
        for g in gz_g[h]:
            g.wait()
        every = g_all[h].reshape(1024, 512)
        here = reduce_me[h]
        red = Reduce(
            lambda s: gw_s.at[h, s - 1],
            row_halves,
            gw_q.at[h],
            gw_r.at[h],
            reduce_at[h],
            gy_ss.at[h],
            gy_rs.at[h],
        )
        for s in (2, 1, 3):
            gw_s[h, s - 1] = dot(ep_t[h, add4(here, s)], every).astype(BF)
            if s == 2:
                red.send_far()
        red.send_near()
        own = dot(ep_t[h, here], every)
        gwk_ref[:, h * DH : (h + 1) * DH] = own[:, 0:256]
        gwv_ref[:, h * DH : (h + 1) * DH] = own[:, 256:512]
        gy_red.append(red)

    scatter(0)

    ge_red.relay()
    scatter(1)
    for red in gy_red:
        red.relay()

    outs = [
        pltpu.make_async_copy(src, dst, out_sem.at[i])
        for i, (src, dst) in enumerate(
            [(gd_ref, gd_hbm), (ge_ref, ge_hbm), (gwk_ref, gwk_hbm), (gwv_ref, gwv_hbm)]
        )
    ]

    for copy in rd_c:
        copy.wait_recv()
    inner = rd_all[0]
    for i in range(1, 8):
        inner = inner + rd_all[i]
    inner = jnp.broadcast_to(inner[0:1, :], (128, 256)).T * (1.0 / D)
    share = pl.ds(pl.multiple_of(mp * 512, 512), 512)
    total = gn_red.total(gn_s[x].astype(F32))
    scaled = total * gain_ref[share].astype(F32).reshape(1, 512)
    rms = rms_v[:, 0:1]
    unit = dec_v[:, share].astype(F32) / rms
    gd_ref[...] = ((scaled - unit * inner[:, 0:1]) / rms).astype(BF)
    outs[0].start()

    total = ge_red.total(ge_s[x].astype(F32))
    back_s[...] = total[0:16, :].reshape(16, 32, 128).astype(BF)
    back_c = [
        remote(back_s.at[peer[0]], back_r.at[dp], back_ss.at[i], back_rs.at[i], peer)
        for i, peer in enumerate(dp_peers)
    ]
    for copy in back_c:
        copy.start()
    back_r[dp] = back_s[dp]
    last = total[16:32, :].astype(BF)

    for h in range(2):
        columns = slice(h * DH, (h + 1) * DH)
        own = jnp.concatenate([gwk_ref[:, columns], gwv_ref[:, columns]], axis=1)
        total = gy_red[h].total(own)
        gwk_ref[:, columns] = total[:, 0:256]
        gwv_ref[:, columns] = total[:, 256:512]

    outs[2].start()
    outs[3].start()
    for copy in back_c:
        copy.wait_recv()
    rows = back_r[...].astype(F32).reshape(16, D).astype(BF)
    rows = jnp.concatenate([rows, last], axis=0)
    ge_ref[...] = dot_tn(perm_v[:, 0:32].astype(BF), rows).astype(BF)
    outs[1].start()
    finish()
    for copy in outs:
        copy.wait()


def hand_on(a, b, c, d, a_out, b_out, c_out, d_out):
    a_out[...] = a[...]
    b_out[...] = b[...]
    c_out[...] = c[...]
    d_out[...] = d[...]


def local(
    enc,
    enc_owner,
    enc_example,
    dec,
    dec_lengths,
    norm_gain,
    w_query,
    w_key,
    w_value,
    w_out,
    grad_out,
):
    vmem = pl.BlockSpec(memory_space=pltpu.VMEM)
    smem = pl.BlockSpec(memory_space=pltpu.SMEM)
    hbm = pl.BlockSpec(memory_space=pl.ANY)
    dma = pltpu.SemaphoreType.DMA
    V = pltpu.VMEM
    shapes = (
        jax.ShapeDtypeStruct((256, 512), BF),
        jax.ShapeDtypeStruct((32, D), BF),
        jax.ShapeDtypeStruct((256, 512), F32),
        jax.ShapeDtypeStruct((256, 512), F32),
    )
    results = pl.pallas_call(
        kernel,
        name="cross_attention_grads",
        out_shape=shapes,
        in_specs=[vmem, smem, smem, smem, vmem] + [hbm] * 6,
        out_specs=(hbm,) * 4,
        scratch_shapes=[
            V((256, 512), BF),
            V((32, D), BF),
            V((256, 512), F32),
            V((256, 512), F32),
            V((256, D), BF),
            V((256, D), BF),
            V((D, 512), BF),
            V((D, 512), BF),
            V((D, 512), BF),
            V((512, D), BF),
            V((8, 32, D + 128), BF),
            V((256, D), BF),
            V((256, 128), F32),
            V((8, 8, 128), F32),
            V((2, 256, 256), BF),
            V((2, 256, 256), BF),
            V((256, 512), BF),
            V((32, 128), F32),
            V((128, 384), BF),
            V((16, 48, 128), F32),
            V((16, 48, 128), BF),
            V((16, 48, 128), BF),
            V((16, 32, 128), BF),
            V((16, 32, 128), BF),
            V((2, 16, 48, 256), BF),
            V((2, 16, 48, 256), BF),
            V((2, 512, 256), BF),
            V((2, 512, 256), BF),
            V((2, 16, 48, 256), BF),
            V((2, 16, 48, 256), BF),
            V((2, 8, 2, 16, 512), BF),
            V((2, 4, 8, 2, 16, 512), BF),
            V((2, 4, 8, 32, 1024), BF),
            V((2, 4, 256, 1024), BF),
            V((2, 3, 256, 512), BF),
            V((2, 2, 256, 512), BF),
            V((2, 2, 128, 512), BF),
            V((4, 2, 256, 512), BF),
            V((4, 256, 512), BF),
            V((4, 256, 512), BF),
            V((2, 256, 512), BF),
            V((2, 128, 512), BF),
            V((2, 4, 32, D), BF),
            V((4, 32, D), BF),
            V((4, 32, D), BF),
            V((2, 32, D), BF),
            V((2, 16, D), BF),
            V((16, 32, 128), BF),
            V((16, 32, 128), BF),
            V((8, 8, 256), F32),
            dma((6,)),
            dma((4,)),
            dma((15,)),
            dma((15,)),
            dma((8,)),
            dma((8,)),
            dma((8,)),
            dma((8,)),
            dma((15,)),
            dma((15,)),
            dma((7,)),
            dma((7,)),
            dma((15,)),
            dma((15,)),
            dma((10,)),
            dma((10,)),
            dma((2, 15)),
            dma((2, 15)),
            dma((2, 15)),
            dma((2, 15)),
            dma((7,)),
            dma((7,)),
            dma((7,)),
            dma((7,)),
            dma((7,)),
            dma((7,)),
            dma((2, 2, 4)),
            dma((2, 2, 4)),
            dma((2, 6)),
            dma((2, 6)),
            dma((15,)),
            dma((15,)),
        ],
        compiler_params=pltpu.CompilerParams(
            collective_id=0, has_side_effects=True, vmem_limit_bytes=60 * 1024 * 1024
        ),
    )(
        enc,
        enc_owner,
        enc_example,
        dec_lengths,
        norm_gain,
        dec,
        grad_out,
        w_query,
        w_key,
        w_value,
        w_out,
    )
    return pl.pallas_call(
        hand_on,
        name="hand_on",
        out_shape=shapes,
        in_specs=[vmem] * 4,
        out_specs=(vmem,) * 4,
    )(*results)


def solution(mesh):
    placed = (
        P(("dp", "mp"), None),
        P(("dp", "mp")),
        P(("dp", "mp")),
        P("dp", None),
        P("dp", None),
        P(),
        P(None, "mp"),
        P(None, "mp"),
        P(None, "mp"),
        P("mp", None),
        P("dp", None),
    )
    return jax.shard_map(
        local,
        mesh=mesh,
        in_specs=placed,
        out_specs=(P("dp", "mp"), P(("dp", "mp"), None), P("dp", "mp"), P("dp", "mp")),
        check_vma=False,
    )
```

```python
import functools

import jax
import jax.numpy as jnp
from jax import lax
from jax.experimental import pallas as pl
from jax.experimental.pallas import tpu as pltpu
from jax.sharding import PartitionSpec as P

MESH = pl.DeviceIdType.MESH
BF = jnp.bfloat16
F32 = jnp.float32
DH = 256
D = 4096
NT = (((1,), (1,)), ((), ()))
TN = (((0,), (0,)), ((), ()))


def dot(a, b):
    return jnp.dot(a, b, preferred_element_type=F32)


def dot_nt(a, b):
    return lax.dot_general(a, b, NT, preferred_element_type=F32)


def dot_tn(a, b):
    return lax.dot_general(a, b, TN, preferred_element_type=F32)


class Copy:
    def __init__(self, copy, started):
        self.copy, self.started, self.received = copy, started, False

    def start(self):
        self.started.append(self)
        self.copy.start()

    def wait_recv(self):
        if not self.received:
            self.received = True
            self.copy.wait_recv()


def add4(value, step):
    return lax.rem(value + step, 4)


def kernel(
    enc_ref,
    owner_ref,
    example_ref,
    len_ref,
    gain_ref,
    dec_hbm,
    go_hbm,
    wq_hbm,
    wk_hbm,
    wv_hbm,
    wo_hbm,
    gd_hbm,
    ge_hbm,
    gwk_hbm,
    gwv_hbm,
    gd_ref,
    ge_ref,
    gwk_ref,
    gwv_ref,
    dec_v,
    go_v,
    wq_v,
    wk_v,
    wv_v,
    wo_v,
    enc_all,
    normed,
    rms_v,
    info_all,
    q_v,
    gc_v,
    gq_v,
    perm_v,
    place_t,
    one_s,
    one_b,
    one_r,
    ex_s,
    ex_r,
    kv_s,
    kv_r,
    key_v,
    value_v,
    ret_s,
    ret_r,
    g_own,
    g_all,
    ep,
    ep_t,
    gw_s,
    gw_r,
    gw_q,
    gn_t,
    gn_sib,
    gn_s,
    gn_r,
    gn_q,
    ge_t,
    ge_sib,
    ge_s,
    ge_r,
    ge_q,
    back_s,
    back_r,
    rd_all,
    load_sem,
    out_sem,
    one_ss,
    one_rs,
    enc_ss,
    enc_rs,
    eno_ss,
    eno_rs,
    ex_ss,
    ex_rs,
    info_ss,
    info_rs,
    epz_ss,
    epz_rs,
    ep_ss,
    ep_rs,
    kv_ss,
    kv_rs,
    ret_ss,
    ret_rs,
    rd_ss,
    rd_rs,
    gn_ss,
    gn_rs,
    ge_ss,
    ge_rs,
    gz_ss,
    gz_rs,
    gy_ss,
    gy_rs,
    back_ss,
    back_rs,
):
    dp = lax.axis_index("dp")
    mp = lax.axis_index("mp")
    y, z = dp // 4, lax.rem(dp, 4)
    x, c = mp // 2, lax.rem(mp, 2)
    other = 1 - c
    sib = (dp, x * 2 + other)

    def at_x(step):
        return (dp, add4(x, step) * 2 + c)

    def at_y(step):
        return (add4(y, step) * 4 + z, mp)

    def at_z(step):
        return (y * 4 + add4(z, step), mp)

    dp_peers = [(lax.rem(dp + i, 16), mp) for i in range(1, 16)]
    mp_peers = [(dp, lax.rem(mp + i, 8)) for i in range(1, 8)]

    started = []

    def remote(src, dst, ss, rs, who):
        copy = pltpu.make_async_remote_copy(
            src_ref=src, dst_ref=dst, send_sem=ss, recv_sem=rs, device_id=who, device_id_type=MESH
        )
        return Copy(copy, started)

    def finish():
        for i in range(6):
            load(i)
        for copy in started:
            copy.wait_recv()
        for copy in started:
            copy.copy.wait_send()

    class Gather:
        def __init__(self, src, slot, halves, place, at, ss, rs):
            self.slot, self.halves, self.place, self.at, self.ss, self.rs = slot, halves, place, at, ss, rs
            self.one = [remote(src, slot(place), ss.at[i], rs.at[i], at(s)) for i, s in enumerate((1, 3))]
            for copy in self.one:
                copy.start()

        def relay(self):
            self.two = []
            for i, s in enumerate((1, 3)):
                self.one[i].wait_recv()
                half = self.halves(self.slot(add4(self.place, 4 - s)))[i]
                copy = remote(half, half, self.ss.at[2 + i], self.rs.at[2 + i], self.at(s))
                copy.start()
                self.two.append(copy)

        def wait(self):
            for copy in self.two:
                copy.wait_recv()

    class Reduce:
        def __init__(self, term, halves, far, got, at, ss, rs):
            self.term, self.halves, self.far, self.got = term, halves, far, got
            self.at, self.ss, self.rs = at, ss, rs
            self.copies = []

        def send(self, src, dst, i, s):
            copy = remote(src, dst, self.ss.at[i], self.rs.at[i], self.at(s))
            copy.start()
            self.copies.append(copy)

        def send_far(self):
            for i, s in enumerate((1, 3)):
                self.send(self.halves(self.term(2))[i], self.far.at[i], i, s)

        def send_near(self):
            for i, s in enumerate((1, 3)):
                self.send(self.halves(self.term(s))[1 - i], self.halves(self.got.at[i])[1 - i], 2 + i, s)

        def relay(self):
            for i, s in enumerate((1, 3)):
                self.copies[i].wait_recv()
                half = self.halves(self.term(s))[i]
                half[...] = (half[...].astype(F32) + self.far[i].astype(F32)).astype(BF)
                self.send(half, self.halves(self.got.at[i])[i], 4 + i, s)

        def total(self, own):
            for copy in self.copies:
                copy.wait_recv()
            return own + self.got[0].astype(F32) + self.got[1].astype(F32)

    loads = [
        pltpu.make_async_copy(src, dst, load_sem.at[i])
        for i, (src, dst) in enumerate(
            [
                (dec_hbm, dec_v),
                (wq_hbm, wq_v),
                (go_hbm, go_v),
                (wo_hbm, wo_v),
                (wk_hbm, wk_v),
                (wv_hbm, wv_v),
            ]
        )
    ]
    for copy in loads:
        copy.start()
    loaded = set()

    def load(i):
        if i not in loaded:
            loaded.add(i)
            loads[i].wait()

    barrier = pltpu.get_barrier_semaphore()
    for peer in dp_peers + mp_peers:
        pl.semaphore_signal(barrier, inc=1, device_id=peer, device_id_type=MESH)

    line = lax.broadcasted_iota(jnp.int32, (8, 128), 0)
    lane = lax.broadcasted_iota(jnp.int32, (8, 128), 1)
    ids = jnp.full((8, 128), -1, jnp.int32)
    for r in range(32):
        ids = jnp.where(lane == r, jnp.where(line == 0, owner_ref[r], example_ref[r]), ids)
    ids = ids.astype(F32)
    owner = ids[0:1, :]
    example = ids[1:2, :] + 1.0
    before = lax.broadcasted_iota(jnp.int32, (128, 128), 0)
    after = lax.broadcasted_iota(jnp.int32, (128, 128), 1)
    upper = jnp.where(before < after, 1.0, 0.0).astype(BF)
    onehot = lax.broadcasted_iota(jnp.int32, (16, 128), 0).astype(F32) == owner
    onehot = jnp.where(onehot, 1.0, 0.0)
    rank = jnp.sum(dot(onehot.astype(BF), upper) * onehot, axis=0, keepdims=True)
    later = jnp.where(rank > 0.5, 1.0, 0.0)
    order = dot(jnp.broadcast_to(later, (16, 128)).astype(BF), upper)[0:1, :]
    position = jnp.where(rank > 0.5, 16.0 + order, owner)
    perm = lax.broadcasted_iota(jnp.int32, (32, 128), 0).astype(F32) == position
    perm = jnp.where(perm, 1.0, 0.0)
    perm_v[...] = perm
    perm = perm[:, 0:32].astype(BF)
    lane_of = jnp.where(rank > 0.5, order + (mp * 16).astype(F32), -1.0)
    moved = jnp.broadcast_to(lane_of, (128, 128)).T == after.astype(F32)
    moved = jnp.where(moved, 1.0, 0.0).astype(BF)
    facts = jnp.where(line == 0, owner, jnp.where(line == 1, rank, example))
    facts = jnp.concatenate([facts, facts], axis=0).astype(BF)
    info_all[mp] = dot(facts, moved)[0:8, :]
    first = jnp.sum(perm_v[0:16, :] * example, axis=1, keepdims=True)
    for i in range(8):
        columns = slice(i * 512, (i + 1) * 512)
        rows = dot(perm, enc_ref[:, columns])
        enc_all[mp, 16:32, columns] = rows[16:32, :].astype(BF)
        one_s[:, i * 4 : (i + 1) * 4, :] = rows[0:16, :].reshape(16, 4, 128)
    one_s[:, 32:48, :] = jnp.broadcast_to(first.reshape(16, 1, 1), (16, 16, 128))
    one_b[...] = one_s[...].astype(BF)

    pl.semaphore_wait(barrier, 22)

    def later_halves(block):
        return block.at[:, 0 : D // 2], block.at[:, D // 2 : D]

    mine = enc_all.at[mp, 16:32, 0:D]
    later_g = Gather(
        mine, lambda place: enc_all.at[place * 2 + c, 16:32, 0:D], later_halves, x, at_x, enc_ss, enc_rs
    )
    one_c = [
        remote(one_b.at[peer[0]], one_r.at[dp], one_ss.at[i], one_rs.at[i], peer)
        for i, peer in enumerate(dp_peers)
    ]
    for copy in one_c:
        copy.start()
    one_r[dp] = one_b[dp]
    info_c = [
        remote(info_all.at[mp], info_all.at[mp], info_ss.at[i], info_rs.at[i], peer)
        for i, peer in enumerate(mp_peers)
    ]
    for copy in info_c:
        copy.start()

    def enc_forward(s):
        block = enc_all.at[add4(x, 4 - s) * 2 + c, 16:32, 0:D]
        return remote(block, block, enc_ss.at[4 + s], enc_rs.at[4 + s], sib)

    enc_f = {s: enc_forward(s) for s in range(4)}
    enc_f[0].start()

    load(0)

    @pl.loop(0, 8)
    def _(i):
        rows = pl.ds(pl.multiple_of(i * 32, 32), 32)
        wide = dec_v[rows, :].astype(F32)
        rms = jnp.sqrt(jnp.mean(wide * wide, axis=-1, keepdims=True) + 1e-06)
        rms_v[rows, :] = jnp.broadcast_to(rms, (32, 128))
        normed[rows, :] = ((wide * (1.0 / rms)) * gain_ref[...].astype(F32).reshape(1, D)).astype(BF)

    later_g.relay()
    for s in (1, 3):
        enc_f[s].start()
    for copy in one_c:
        copy.wait_recv()
    rows = one_r[...].astype(F32)
    enc_all[mp, 0:16, 0:D] = rows[:, 0:32, :].reshape(16, D).astype(BF)
    enc_all[mp, 0:16, D : D + 128] = rows[:, 32, :].astype(BF)
    def first_halves(block):
        return block.at[:, 0 : D // 2], block.at[:, D // 2 : D + 128]

    first_g = Gather(
        enc_all.at[mp, 0:16, :],
        lambda place: enc_all.at[place * 2 + c, 0:16, :],
        first_halves,
        x,
        at_x,
        eno_ss,
        eno_rs,
    )

    def eno_forward(s):
        block = enc_all.at[add4(x, 4 - s) * 2 + c, 0:16, :]
        return remote(block, block, eno_ss.at[4 + s], eno_rs.at[4 + s], sib)

    eno_f = {s: eno_forward(s) for s in range(4)}
    eno_f[0].start()
    epz = []
    for s in (1, 2, 3):
        for b in range(4):
            column = pl.multiple_of((b * 4 + add4(z, s)) * 256, 256)
            epz.append(
                remote(
                    enc_all.at[mp, :, pl.ds(column, 256)],
                    ep.at[0, z, mp, :, pl.ds(b * 256, 256)],
                    epz_ss.at[(s - 1) * 4 + b],
                    epz_rs.at[(s - 1) * 4 + b],
                    at_z(s),
                )
            )
        column = pl.multiple_of(add4(y, s) * 1024, 1024)
        epz.append(
            remote(
                enc_all.at[mp, :, pl.ds(column, 1024)],
                ep.at[1, y, mp],
                epz_ss.at[11 + s],
                epz_rs.at[11 + s],
                at_y(s),
            )
        )
    for copy in epz:
        copy.start()
    for b in range(4):
        column = pl.multiple_of((b * 4 + z) * 256, 256)
        ep[0, z, mp, :, pl.ds(b * 256, 256)] = enc_all[mp, :, pl.ds(column, 256)]
    ep[1, y, mp] = enc_all[mp, :, pl.ds(pl.multiple_of(y * 1024, 1024), 1024)]

    def gc_and_first():
        load(2)
        load(3)
        for h in range(2):
            gc_v[h] = dot_nt(go_v[...], wo_v[h * DH : (h + 1) * DH, :]).astype(BF)
        for s in range(4):
            eno_f[s].wait_recv()
        rows = enc_all[:, 0:16, 0:D].reshape(128, D)
        for h in range(2):
            columns = slice(h * DH, (h + 1) * DH)
            key_v[h, 0:128, :] = dot(rows, wk_v[:, columns]).astype(BF)
            value_v[h, 0:128, :] = dot(rows, wv_v[:, columns]).astype(BF)

    for copy in info_c:
        copy.wait_recv()
    info = info_all[0]
    for i in range(1, 8):
        info = info + info_all[i]
    block = lax.shift_right_logical(lax.broadcasted_iota(jnp.int32, (1, 128), 1), 4).astype(F32)
    target = info[0:1, :] * 24.0 + block * 3.0 + info[1:2, :] - 1.0
    slot_id = lax.broadcasted_iota(jnp.int32, (384, 128), 0).astype(F32)
    placed = jnp.where(slot_id == target, 1.0, 0.0)
    place = placed.astype(BF)
    place_t[...] = placed.T.astype(BF)
    slot_example = jnp.sum(placed * info[2:3, :], axis=1, keepdims=True)
    slot_example = jnp.broadcast_to(slot_example, (384, 128)).reshape(16, 24, 128)
    ex_s[...] = jnp.concatenate([slot_example, jnp.zeros((16, 8, 128), F32)], axis=1).astype(BF)
    ex_c = [
        remote(ex_s.at[peer[0]], ex_r.at[dp], ex_ss.at[i], ex_rs.at[i], peer)
        for i, peer in enumerate(dp_peers)
    ]
    for copy in ex_c:
        copy.start()
    ex_r[dp] = ex_s[dp]

    later_g.wait()
    enc_f[2].start()
    load(1)
    for h in range(2):
        q_v[h] = dot(normed[...], wq_v[:, h * DH : (h + 1) * DH]).astype(BF)
    for s in range(4):
        enc_f[s].wait_recv()
    load(4)
    load(5)
    kv_c = []
    for h in range(2):
        columns = slice(h * DH, (h + 1) * DH)
        rows = enc_all[:, 16:32, 0:D].reshape(128, D)
        key = dot(place, dot(rows, wk_v[:, columns]).astype(BF)).reshape(16, 24, 256)
        value = dot(place, dot(rows, wv_v[:, columns]).astype(BF)).reshape(16, 24, 256)
        kv_s[h] = jnp.concatenate([key, value], axis=1).astype(BF)
        copies = [
            remote(kv_s.at[h, peer[0]], kv_r.at[h, dp], kv_ss.at[h, i], kv_rs.at[h, i], peer)
            for i, peer in enumerate(dp_peers)
        ]
        for copy in copies:
            copy.start()
        kv_r[h, dp] = kv_s[h, dp]
        kv_c.append(copies)
        if h == 0:
            first_g.relay()
            for s in (1, 3):
                eno_f[s].start()

    first_g.wait()
    eno_f[2].start()
    for copy in epz:
        copy.wait_recv()
    ep_g = Gather(
        ep.at[:, :, mp],
        lambda place: ep.at[:, :, place * 2 + c],
        lambda block: (block.at[0], block.at[1]),
        x,
        at_x,
        ep_ss,
        ep_rs,
    )

    def ep_forward(s):
        block = ep.at[:, :, add4(x, 4 - s) * 2 + c]
        return remote(block, block, ep_ss.at[4 + s], ep_rs.at[4 + s], sib)

    ep_f = {s: ep_forward(s) for s in range(4)}
    ep_f[0].start()

    gc_and_first()

    place_of = lax.broadcasted_iota(jnp.int32, (1, 256), 1)
    bound = jnp.int32(0)
    segment = jnp.zeros((1, 256), jnp.int32)
    for e in range(8):
        bound = bound + len_ref[0, e]
        segment = segment + jnp.where(bound <= place_of, 1, 0)
    segment = segment.astype(F32) + 1.0

    scale = DH**-0.5
    ret_c = []
    gz_g = [[], []]
    gather_at, reduce_at = [at_z, at_y], [at_y, at_z]
    gather_me, reduce_me = [z, y], [y, z]

    def gather(h, part):
        here = gather_me[h]
        g_all[h, here, :, part] = g_own[h, :, part]
        gz_g[h].append(
            Gather(
                g_own.at[h, :, part],
                lambda place: g_all.at[h, place, :, part],
                lambda block: (block.at[0:4], block.at[4:8]),
                here,
                gather_at[h],
                gz_ss.at[h, part],
                gz_rs.at[h, part],
            )
        )

    row_dot = jnp.zeros((1, 256), F32)
    for copy in ex_c:
        copy.wait_recv()
    ex = enc_all[:, 0:16, D : D + 128].reshape(128, 128).astype(F32)
    ex = jnp.concatenate([ex, ex_r[...].astype(F32)[:, 0:24, :].reshape(384, 128)], axis=0)
    allowed = jnp.concatenate([ex, ex], axis=1) == segment
    for h in range(2):
        for copy in kv_c[h]:
            copy.wait_recv()
        both = kv_r[h].astype(F32)
        key_v[h, 128:512, :] = both[:, 0:24, :].reshape(384, 256).astype(BF)
        value_v[h, 128:512, :] = both[:, 24:48, :].reshape(384, 256).astype(BF)
        key = key_v[h]
        value = value_v[h]
        raw = dot_nt(key, q_v[h])
        scores = jnp.where(allowed, raw * scale, -1e30)
        top = jnp.max(scores, axis=0, keepdims=True)
        weights = jnp.where(allowed, jnp.exp(scores - top), 0.0)
        probs = weights / jnp.sum(weights, axis=0, keepdims=True)
        grad_probs = dot_nt(value, gc_v[h])
        inner = jnp.sum(probs * grad_probs, axis=0, keepdims=True)
        grad_scores = (probs * (grad_probs - inner) * scale).astype(BF)
        row_dot = row_dot + jnp.sum(grad_scores.astype(F32) * raw, axis=0, keepdims=True)
        grad_key = dot(grad_scores, q_v[h])
        grad_value = dot(probs.astype(BF), gc_v[h])
        ret_s[h] = jnp.concatenate(
            [grad_key[128:512, :].reshape(16, 24, 256), grad_value[128:512, :].reshape(16, 24, 256)],
            axis=1,
        ).astype(BF)
        copies = [
            remote(ret_s.at[h, peer[0]], ret_r.at[h, dp], ret_ss.at[h, i], ret_rs.at[h, i], peer)
            for i, peer in enumerate(dp_peers)
        ]
        for copy in copies:
            copy.start()
        ret_c.append(copies)
        ret_r[h, dp] = ret_s[h, dp]
        g_own[h, :, 0, :, 0:256] = grad_key[0:128, :].astype(BF).reshape(8, 16, 256)
        g_own[h, :, 0, :, 256:512] = grad_value[0:128, :].astype(BF).reshape(8, 16, 256)
        gather(h, 0)
        gq_v[:, h * DH : (h + 1) * DH] = dot_tn(grad_scores, key).astype(BF)

    rd_all[mp] = jnp.broadcast_to(row_dot, (8, 256))
    rd_c = [
        remote(rd_all.at[mp], rd_all.at[mp], rd_ss.at[i], rd_rs.at[i], peer)
        for i, peer in enumerate(mp_peers)
    ]
    for copy in rd_c:
        copy.start()

    def take_back(h):
        for copy in ret_c[h]:
            copy.wait_recv()
        both = ret_r[h].astype(F32)
        for k in range(2):
            back = both[:, k * 24 : (k + 1) * 24, :].reshape(384, 256).astype(BF)
            back = dot(place_t[...], back).astype(BF).reshape(8, 16, 256)
            g_own[h, :, 1, :, k * 256 : (k + 1) * 256] = back
        gather(h, 1)

    def row_halves(block):
        return block.at[0:128], block.at[128:256]

    def column_halves(block):
        return block.at[:, 0 : D // 2], block.at[:, D // 2 : D]

    @pl.loop(0, 4)
    def _(i):
        for k in range(2):
            rows = pl.ds(pl.multiple_of((i * 2 + k) * 512, 512), 512)
            gn_t[i, k] = dot_nt(gq_v[...], wq_v[rows, :]).astype(BF)

    gn_pair = remote(gn_t.at[:, other], gn_sib, gn_ss.at[6], gn_rs.at[6], sib)
    gn_pair.start()

    ge_pair = []

    def enc_term(part):
        @pl.loop(0, 8)
        def _(i):
            rows = pl.ds(pl.multiple_of(i * 512, 512), 512)
            total = jnp.zeros((128, 512), F32)
            for h in range(2):
                own = g_own[h, :, part].reshape(128, 512)
                total = total + dot_nt(own[:, 0:256], wk_v[rows, h * DH : (h + 1) * DH])
                total = total + dot_nt(own[:, 256:512], wv_v[rows, h * DH : (h + 1) * DH])
            total = total.astype(BF).reshape(4, 2, 16, 512)
            for k in range(2):
                ge_t[part, k, :, :, rows] = total[:, k]

        pair = remote(
            ge_t.at[part, other], ge_sib.at[part], ge_ss.at[part, 6], ge_rs.at[part, 6], sib
        )
        pair.start()
        ge_pair.append(pair)

    ge_red = []

    def enc_reduce(part):
        ge_pair[part].wait_recv()

        @pl.loop(0, 4)
        def _(i):
            ge_s[part, i] = (ge_t[part, c, i].astype(F32) + ge_sib[part, i].astype(F32)).astype(BF)

        red = Reduce(
            lambda s: ge_s.at[part, add4(x, s)],
            column_halves,
            ge_q.at[part],
            ge_r.at[part],
            at_x,
            ge_ss.at[part],
            ge_rs.at[part],
        )
        red.send_far()
        red.send_near()
        ge_red.append(red)

    ep_g.relay()
    for s in (1, 3):
        ep_f[s].start()
    enc_term(0)
    gn_pair.wait_recv()

    @pl.loop(0, 4)
    def _(i):
        gn_s[i] = (gn_t[i, c].astype(F32) + gn_sib[i].astype(F32)).astype(BF)

    gn_red = Reduce(lambda s: gn_s.at[add4(x, s)], row_halves, gn_q, gn_r, at_x, gn_ss, gn_rs)
    gn_red.send_far()
    gn_red.send_near()
    for h in range(2):
        gz_g[h][0].relay()
    enc_reduce(0)
    take_back(0)
    take_back(1)
    enc_term(1)
    for h in range(2):
        gz_g[h][1].relay()
    ep_g.wait()
    ep_f[2].start()
    gn_red.relay()
    enc_reduce(1)

    for s in range(4):
        ep_f[s].wait_recv()
    for h in range(2):
        for b in range(4):
            for k in range(4):
                part = ep[h, k, :, :, b * 256 : (b + 1) * 256].reshape(256, 256)
                ep_t[h, b, :, k * 256 : (k + 1) * 256] = part.T
    ge_red[0].relay()

    gy_red = []

    def scatter(h):
        for g in gz_g[h]:
            g.wait()
        every = g_all[h].reshape(1024, 512)
        here = reduce_me[h]
        red = Reduce(
            lambda s: gw_s.at[h, s - 1],
            row_halves,
            gw_q.at[h],
            gw_r.at[h],
            reduce_at[h],
            gy_ss.at[h],
            gy_rs.at[h],
        )
        for s in (2, 1, 3):
            gw_s[h, s - 1] = dot(ep_t[h, add4(here, s)], every).astype(BF)
            if s == 2:
                red.send_far()
        red.send_near()
        own = dot(ep_t[h, here], every)
        gwk_ref[:, h * DH : (h + 1) * DH] = own[:, 0:256]
        gwv_ref[:, h * DH : (h + 1) * DH] = own[:, 256:512]
        gy_red.append(red)

    scatter(0)

    scatter(1)
    ge_red[1].relay()
    for red in gy_red:
        red.relay()

    outs = [
        pltpu.make_async_copy(src, dst, out_sem.at[i])
        for i, (src, dst) in enumerate(
            [(gd_ref, gd_hbm), (ge_ref, ge_hbm), (gwk_ref, gwk_hbm), (gwv_ref, gwv_hbm)]
        )
    ]

    total = ge_red[0].total(ge_s[0, x].astype(F32))
    back_s[...] = total.reshape(16, 32, 128).astype(BF)
    back_c = [
        remote(back_s.at[peer[0]], back_r.at[dp], back_ss.at[i], back_rs.at[i], peer)
        for i, peer in enumerate(dp_peers)
    ]
    for copy in back_c:
        copy.start()
    back_r[dp] = back_s[dp]

    for copy in rd_c:
        copy.wait_recv()
    inner = rd_all[0]
    for i in range(1, 8):
        inner = inner + rd_all[i]
    inner = jnp.broadcast_to(inner[0:1, :], (128, 256)).T * (1.0 / D)
    share = pl.ds(pl.multiple_of(mp * 512, 512), 512)
    total = gn_red.total(gn_s[x].astype(F32))
    scaled = total * gain_ref[share].astype(F32).reshape(1, 512)
    rms = rms_v[:, 0:1]
    unit = dec_v[:, share].astype(F32) / rms
    gd_ref[...] = ((scaled - unit * inner[:, 0:1]) / rms).astype(BF)
    outs[0].start()

    for h in range(2):
        columns = slice(h * DH, (h + 1) * DH)
        own = jnp.concatenate([gwk_ref[:, columns], gwv_ref[:, columns]], axis=1)
        total = gy_red[h].total(own)
        gwk_ref[:, columns] = total[:, 0:256]
        gwv_ref[:, columns] = total[:, 256:512]

    outs[2].start()
    outs[3].start()
    last = ge_red[1].total(ge_s[1, x].astype(F32)).astype(BF)
    for copy in back_c:
        copy.wait_recv()
    rows = back_r[...].astype(F32).reshape(16, D).astype(BF)
    rows = jnp.concatenate([rows, last], axis=0)
    ge_ref[...] = dot_tn(perm_v[:, 0:32].astype(BF), rows).astype(BF)
    outs[1].start()
    finish()
    for copy in outs:
        copy.wait()


def hand_on(a, b, c, d, a_out, b_out, c_out, d_out):
    a_out[...] = a[...]
    b_out[...] = b[...]
    c_out[...] = c[...]
    d_out[...] = d[...]


def local(
    enc,
    enc_owner,
    enc_example,
    dec,
    dec_lengths,
    norm_gain,
    w_query,
    w_key,
    w_value,
    w_out,
    grad_out,
):
    vmem = pl.BlockSpec(memory_space=pltpu.VMEM)
    smem = pl.BlockSpec(memory_space=pltpu.SMEM)
    hbm = pl.BlockSpec(memory_space=pl.ANY)
    dma = pltpu.SemaphoreType.DMA
    V = pltpu.VMEM
    shapes = (
        jax.ShapeDtypeStruct((256, 512), BF),
        jax.ShapeDtypeStruct((32, D), BF),
        jax.ShapeDtypeStruct((256, 512), F32),
        jax.ShapeDtypeStruct((256, 512), F32),
    )
    results = pl.pallas_call(
        kernel,
        name="cross_attention_grads",
        out_shape=shapes,
        in_specs=[vmem, smem, smem, smem, vmem] + [hbm] * 6,
        out_specs=(hbm,) * 4,
        scratch_shapes=[
            V((256, 512), BF),
            V((32, D), BF),
            V((256, 512), F32),
            V((256, 512), F32),
            V((256, D), BF),
            V((256, D), BF),
            V((D, 512), BF),
            V((D, 512), BF),
            V((D, 512), BF),
            V((512, D), BF),
            V((8, 32, D + 128), BF),
            V((256, D), BF),
            V((256, 128), F32),
            V((8, 8, 128), F32),
            V((2, 256, 256), BF),
            V((2, 256, 256), BF),
            V((256, 512), BF),
            V((32, 128), F32),
            V((128, 384), BF),
            V((16, 48, 128), F32),
            V((16, 48, 128), BF),
            V((16, 48, 128), BF),
            V((16, 32, 128), BF),
            V((16, 32, 128), BF),
            V((2, 16, 48, 256), BF),
            V((2, 16, 48, 256), BF),
            V((2, 512, 256), BF),
            V((2, 512, 256), BF),
            V((2, 16, 48, 256), BF),
            V((2, 16, 48, 256), BF),
            V((2, 8, 2, 16, 512), BF),
            V((2, 4, 8, 2, 16, 512), BF),
            V((2, 4, 8, 32, 1024), BF),
            V((2, 4, 256, 1024), BF),
            V((2, 3, 256, 512), BF),
            V((2, 2, 256, 512), BF),
            V((2, 2, 128, 512), BF),
            V((4, 2, 256, 512), BF),
            V((4, 256, 512), BF),
            V((4, 256, 512), BF),
            V((2, 256, 512), BF),
            V((2, 128, 512), BF),
            V((2, 2, 4, 16, D), BF),
            V((2, 4, 16, D), BF),
            V((2, 4, 16, D), BF),
            V((2, 2, 16, D), BF),
            V((2, 2, 16, D // 2), BF),
            V((16, 32, 128), BF),
            V((16, 32, 128), BF),
            V((8, 8, 256), F32),
            dma((6,)),
            dma((4,)),
            dma((15,)),
            dma((15,)),
            dma((8,)),
            dma((8,)),
            dma((8,)),
            dma((8,)),
            dma((15,)),
            dma((15,)),
            dma((7,)),
            dma((7,)),
            dma((15,)),
            dma((15,)),
            dma((10,)),
            dma((10,)),
            dma((2, 15)),
            dma((2, 15)),
            dma((2, 15)),
            dma((2, 15)),
            dma((7,)),
            dma((7,)),
            dma((7,)),
            dma((7,)),
            dma((2, 7)),
            dma((2, 7)),
            dma((2, 2, 4)),
            dma((2, 2, 4)),
            dma((2, 6)),
            dma((2, 6)),
            dma((15,)),
            dma((15,)),
        ],
        compiler_params=pltpu.CompilerParams(
            collective_id=0, has_side_effects=True, vmem_limit_bytes=60 * 1024 * 1024
        ),
    )(
        enc,
        enc_owner,
        enc_example,
        dec_lengths,
        norm_gain,
        dec,
        grad_out,
        w_query,
        w_key,
        w_value,
        w_out,
    )
    return pl.pallas_call(
        hand_on,
        name="hand_on",
        out_shape=shapes,
        in_specs=[vmem] * 4,
        out_specs=(vmem,) * 4,
    )(*results)


def solution(mesh):
    placed = (
        P(("dp", "mp"), None),
        P(("dp", "mp")),
        P(("dp", "mp")),
        P("dp", None),
        P("dp", None),
        P(),
        P(None, "mp"),
        P(None, "mp"),
        P(None, "mp"),
        P("mp", None),
        P("dp", None),
    )
    return jax.shard_map(
        local,
        mesh=mesh,
        in_specs=placed,
        out_specs=(P("dp", "mp"), P(("dp", "mp"), None), P("dp", "mp"), P("dp", "mp")),
        check_vma=False,
    )
```

```python
import functools

import jax
import jax.numpy as jnp
from jax import lax
from jax.experimental import pallas as pl
from jax.experimental.pallas import tpu as pltpu
from jax.sharding import PartitionSpec as P

MESH = pl.DeviceIdType.MESH
BF = jnp.bfloat16
F32 = jnp.float32
DH = 256
D = 4096
NT = (((1,), (1,)), ((), ()))
TN = (((0,), (0,)), ((), ()))


def dot(a, b):
    return jnp.dot(a, b, preferred_element_type=F32)


def dot_nt(a, b):
    return lax.dot_general(a, b, NT, preferred_element_type=F32)


def dot_tn(a, b):
    return lax.dot_general(a, b, TN, preferred_element_type=F32)


class Copy:
    def __init__(self, copy, started):
        self.copy, self.started, self.received = copy, started, False

    def start(self):
        self.started.append(self)
        self.copy.start()

    def wait_recv(self):
        if not self.received:
            self.received = True
            self.copy.wait_recv()


def add4(value, step):
    return lax.rem(value + step, 4)


def kernel(
    enc_hbm,
    owner_ref,
    example_ref,
    len_ref,
    gain_ref,
    dec_hbm,
    go_hbm,
    wq_hbm,
    wk_hbm,
    wv_hbm,
    wo_hbm,
    gd_hbm,
    ge_hbm,
    gwk_hbm,
    gwv_hbm,
    gd_ref,
    ge_ref,
    gwk_ref,
    gwv_ref,
    enc_ref,
    dec_v,
    go_v,
    wq_v,
    wk_v,
    wv_v,
    wo_v,
    enc_all,
    normed,
    rms_v,
    info_all,
    q_v,
    gc_v,
    gq_v,
    perm_v,
    place_t,
    one_s,
    one_b,
    one_r,
    ex_s,
    ex_r,
    kv_s,
    kv_r,
    key_v,
    value_v,
    ret_s,
    ret_r,
    g_own,
    g_all,
    ep,
    ep_t,
    gw_s,
    gw_r,
    gw_q,
    gn_t,
    gn_sib,
    gn_s,
    gn_r,
    gn_q,
    ge_t,
    ge_sib,
    ge_s,
    ge_r,
    ge_q,
    back_s,
    back_r,
    rd_all,
    load_sem,
    out_sem,
    one_ss,
    one_rs,
    enc_ss,
    enc_rs,
    eno_ss,
    eno_rs,
    ex_ss,
    ex_rs,
    info_ss,
    info_rs,
    epz_ss,
    epz_rs,
    ep_ss,
    ep_rs,
    kv_ss,
    kv_rs,
    ret_ss,
    ret_rs,
    rd_ss,
    rd_rs,
    gn_ss,
    gn_rs,
    ge_ss,
    ge_rs,
    gz_ss,
    gz_rs,
    gy_ss,
    gy_rs,
    back_ss,
    back_rs,
):
    dp = lax.axis_index("dp")
    mp = lax.axis_index("mp")
    y, z = dp // 4, lax.rem(dp, 4)
    x, c = mp // 2, lax.rem(mp, 2)
    other = 1 - c
    sib = (dp, x * 2 + other)

    def at_x(step):
        return (dp, add4(x, step) * 2 + c)

    def at_y(step):
        return (add4(y, step) * 4 + z, mp)

    def at_z(step):
        return (y * 4 + add4(z, step), mp)

    dp_peers = [(lax.rem(dp + i, 16), mp) for i in range(1, 16)]
    mp_peers = [(dp, lax.rem(mp + i, 8)) for i in range(1, 8)]

    barrier = pltpu.get_barrier_semaphore()
    for peer in dp_peers + mp_peers:
        pl.semaphore_signal(barrier, inc=1, device_id=peer, device_id_type=MESH)

    started = []

    def remote(src, dst, ss, rs, who):
        copy = pltpu.make_async_remote_copy(
            src_ref=src, dst_ref=dst, send_sem=ss, recv_sem=rs, device_id=who, device_id_type=MESH
        )
        return Copy(copy, started)

    def finish():
        for i in range(7):
            load(i)
        for copy in started:
            copy.wait_recv()
        for copy in started:
            copy.copy.wait_send()

    class Gather:
        def __init__(self, src, slot, halves, place, at, ss, rs):
            self.slot, self.halves, self.place, self.at, self.ss, self.rs = slot, halves, place, at, ss, rs
            self.one = [remote(src, slot(place), ss.at[i], rs.at[i], at(s)) for i, s in enumerate((1, 3))]
            for copy in self.one:
                copy.start()

        def relay(self):
            self.two = []
            for i, s in enumerate((1, 3)):
                self.one[i].wait_recv()
                half = self.halves(self.slot(add4(self.place, 4 - s)))[i]
                copy = remote(half, half, self.ss.at[2 + i], self.rs.at[2 + i], self.at(s))
                copy.start()
                self.two.append(copy)

        def wait(self):
            for copy in self.two:
                copy.wait_recv()

    class Reduce:
        def __init__(self, term, halves, far, got, at, ss, rs):
            self.term, self.halves, self.far, self.got = term, halves, far, got
            self.at, self.ss, self.rs = at, ss, rs
            self.copies = []

        def send(self, src, dst, i, s):
            copy = remote(src, dst, self.ss.at[i], self.rs.at[i], self.at(s))
            copy.start()
            self.copies.append(copy)

        def send_far(self):
            for i, s in enumerate((1, 3)):
                self.send(self.halves(self.term(2))[i], self.far.at[i], i, s)

        def send_near(self):
            for i, s in enumerate((1, 3)):
                self.send(self.halves(self.term(s))[1 - i], self.halves(self.got.at[i])[1 - i], 2 + i, s)

        def relay(self):
            for i, s in enumerate((1, 3)):
                self.copies[i].wait_recv()
                half = self.halves(self.term(s))[i]
                half[...] = (half[...].astype(F32) + self.far[i].astype(F32)).astype(BF)
                self.send(half, self.halves(self.got.at[i])[i], 4 + i, s)

        def total(self, own):
            for copy in self.copies:
                copy.wait_recv()
            return own + self.got[0].astype(F32) + self.got[1].astype(F32)

    loads = [
        pltpu.make_async_copy(src, dst, load_sem.at[i])
        for i, (src, dst) in enumerate(
            [
                (dec_hbm, dec_v),
                (wq_hbm, wq_v),
                (go_hbm, go_v),
                (wo_hbm, wo_v),
                (wk_hbm, wk_v),
                (wv_hbm, wv_v),
                (enc_hbm, enc_ref),
            ]
        )
    ]
    for i in (6, 0, 1, 4, 5, 2, 3):
        loads[i].start()
    loaded = set()

    def load(i):
        if i not in loaded:
            loaded.add(i)
            loads[i].wait()

    line = lax.broadcasted_iota(jnp.int32, (8, 128), 0)
    lane = lax.broadcasted_iota(jnp.int32, (8, 128), 1)
    ids = jnp.full((8, 128), -1, jnp.int32)
    for r in range(32):
        ids = jnp.where(lane == r, jnp.where(line == 0, owner_ref[r], example_ref[r]), ids)
    ids = ids.astype(F32)
    owner = ids[0:1, :]
    example = ids[1:2, :] + 1.0
    before = lax.broadcasted_iota(jnp.int32, (128, 128), 0)
    after = lax.broadcasted_iota(jnp.int32, (128, 128), 1)
    upper = jnp.where(before < after, 1.0, 0.0).astype(BF)
    onehot = lax.broadcasted_iota(jnp.int32, (16, 128), 0).astype(F32) == owner
    onehot = jnp.where(onehot, 1.0, 0.0)
    rank = jnp.sum(dot(onehot.astype(BF), upper) * onehot, axis=0, keepdims=True)
    later = jnp.where(rank > 0.5, 1.0, 0.0)
    order = dot(jnp.broadcast_to(later, (16, 128)).astype(BF), upper)[0:1, :]
    position = jnp.where(rank > 0.5, 16.0 + order, owner)
    perm = lax.broadcasted_iota(jnp.int32, (32, 128), 0).astype(F32) == position
    perm = jnp.where(perm, 1.0, 0.0)
    perm_v[...] = perm
    perm = perm[:, 0:32].astype(BF)
    lane_of = jnp.where(rank > 0.5, order + (mp * 16).astype(F32), -1.0)
    moved = jnp.broadcast_to(lane_of, (128, 128)).T == after.astype(F32)
    moved = jnp.where(moved, 1.0, 0.0).astype(BF)
    facts = jnp.where(line == 0, owner, jnp.where(line == 1, rank, example))
    facts = jnp.concatenate([facts, facts], axis=0).astype(BF)
    info_all[mp] = dot(facts, moved)[0:8, :]
    first = jnp.sum(perm_v[0:16, :] * example, axis=1, keepdims=True)
    load(6)
    for i in range(8):
        columns = slice(i * 512, (i + 1) * 512)
        rows = dot(perm, enc_ref[:, columns])
        enc_all[mp, 16:32, columns] = rows[16:32, :].astype(BF)
        one_s[:, i * 4 : (i + 1) * 4, :] = rows[0:16, :].reshape(16, 4, 128)
    one_s[:, 32:48, :] = jnp.broadcast_to(first.reshape(16, 1, 1), (16, 16, 128))
    one_b[...] = one_s[...].astype(BF)

    pl.semaphore_wait(barrier, 22)

    def later_halves(block):
        return block.at[:, 0 : D // 2], block.at[:, D // 2 : D]

    mine = enc_all.at[mp, 16:32, 0:D]
    later_g = Gather(
        mine, lambda place: enc_all.at[place * 2 + c, 16:32, 0:D], later_halves, x, at_x, enc_ss, enc_rs
    )
    one_c = [
        remote(one_b.at[peer[0]], one_r.at[dp], one_ss.at[i], one_rs.at[i], peer)
        for i, peer in enumerate(dp_peers)
    ]
    for copy in one_c:
        copy.start()
    one_r[dp] = one_b[dp]
    info_c = [
        remote(info_all.at[mp], info_all.at[mp], info_ss.at[i], info_rs.at[i], peer)
        for i, peer in enumerate(mp_peers)
    ]
    for copy in info_c:
        copy.start()

    def enc_forward(s):
        block = enc_all.at[add4(x, 4 - s) * 2 + c, 16:32, 0:D]
        return remote(block, block, enc_ss.at[4 + s], enc_rs.at[4 + s], sib)

    enc_f = {s: enc_forward(s) for s in range(4)}
    enc_f[0].start()

    load(0)

    @pl.loop(0, 8)
    def _(i):
        rows = pl.ds(pl.multiple_of(i * 32, 32), 32)
        wide = dec_v[rows, :].astype(F32)
        rms = jnp.sqrt(jnp.mean(wide * wide, axis=-1, keepdims=True) + 1e-06)
        rms_v[rows, :] = jnp.broadcast_to(rms, (32, 128))
        normed[rows, :] = ((wide * (1.0 / rms)) * gain_ref[...].astype(F32).reshape(1, D)).astype(BF)

    load(1)
    for h in range(2):
        q_v[h] = dot(normed[...], wq_v[:, h * DH : (h + 1) * DH]).astype(BF)
    later_g.relay()
    for s in (1, 3):
        enc_f[s].start()
    for copy in one_c:
        copy.wait_recv()
    rows = one_r[...].astype(F32)
    enc_all[mp, 0:16, 0:D] = rows[:, 0:32, :].reshape(16, D).astype(BF)
    enc_all[mp, 0:16, D : D + 128] = rows[:, 32, :].astype(BF)
    def first_halves(block):
        return block.at[:, 0 : D // 2], block.at[:, D // 2 : D + 128]

    first_g = Gather(
        enc_all.at[mp, 0:16, :],
        lambda place: enc_all.at[place * 2 + c, 0:16, :],
        first_halves,
        x,
        at_x,
        eno_ss,
        eno_rs,
    )

    def eno_forward(s):
        block = enc_all.at[add4(x, 4 - s) * 2 + c, 0:16, :]
        return remote(block, block, eno_ss.at[4 + s], eno_rs.at[4 + s], sib)

    eno_f = {s: eno_forward(s) for s in range(4)}
    eno_f[0].start()
    epz = []
    for s in (1, 2, 3):
        for b in range(4):
            column = pl.multiple_of((b * 4 + add4(z, s)) * 256, 256)
            epz.append(
                remote(
                    enc_all.at[mp, :, pl.ds(column, 256)],
                    ep.at[0, z, mp, :, pl.ds(b * 256, 256)],
                    epz_ss.at[(s - 1) * 4 + b],
                    epz_rs.at[(s - 1) * 4 + b],
                    at_z(s),
                )
            )
        column = pl.multiple_of(add4(y, s) * 1024, 1024)
        epz.append(
            remote(
                enc_all.at[mp, :, pl.ds(column, 1024)],
                ep.at[1, y, mp],
                epz_ss.at[11 + s],
                epz_rs.at[11 + s],
                at_y(s),
            )
        )
    for copy in epz:
        copy.start()
    for b in range(4):
        column = pl.multiple_of((b * 4 + z) * 256, 256)
        ep[0, z, mp, :, pl.ds(b * 256, 256)] = enc_all[mp, :, pl.ds(column, 256)]
    ep[1, y, mp] = enc_all[mp, :, pl.ds(pl.multiple_of(y * 1024, 1024), 1024)]

    def gc_and_first():
        load(2)
        load(3)
        for h in range(2):
            gc_v[h] = dot_nt(go_v[...], wo_v[h * DH : (h + 1) * DH, :]).astype(BF)
        for s in range(4):
            eno_f[s].wait_recv()
        rows = enc_all[:, 0:16, 0:D].reshape(128, D)
        for h in range(2):
            columns = slice(h * DH, (h + 1) * DH)
            key_v[h, 0:128, :] = dot(rows, wk_v[:, columns]).astype(BF)
            value_v[h, 0:128, :] = dot(rows, wv_v[:, columns]).astype(BF)

    for copy in info_c:
        copy.wait_recv()
    info = info_all[0]
    for i in range(1, 8):
        info = info + info_all[i]
    block = lax.shift_right_logical(lax.broadcasted_iota(jnp.int32, (1, 128), 1), 4).astype(F32)
    target = info[0:1, :] * 24.0 + block * 3.0 + info[1:2, :] - 1.0
    slot_id = lax.broadcasted_iota(jnp.int32, (384, 128), 0).astype(F32)
    placed = jnp.where(slot_id == target, 1.0, 0.0)
    place = placed.astype(BF)
    place_t[...] = placed.T.astype(BF)
    slot_example = jnp.sum(placed * info[2:3, :], axis=1, keepdims=True)
    slot_example = jnp.broadcast_to(slot_example, (384, 128)).reshape(16, 24, 128)
    ex_s[...] = jnp.concatenate([slot_example, jnp.zeros((16, 8, 128), F32)], axis=1).astype(BF)
    ex_c = [
        remote(ex_s.at[peer[0]], ex_r.at[dp], ex_ss.at[i], ex_rs.at[i], peer)
        for i, peer in enumerate(dp_peers)
    ]
    for copy in ex_c:
        copy.start()
    ex_r[dp] = ex_s[dp]

    later_g.wait()
    enc_f[2].start()
    for s in range(4):
        enc_f[s].wait_recv()
    load(4)
    load(5)
    kv_c = []
    for h in range(2):
        columns = slice(h * DH, (h + 1) * DH)
        rows = enc_all[:, 16:32, 0:D].reshape(128, D)
        key = dot(place, dot(rows, wk_v[:, columns]).astype(BF)).reshape(16, 24, 256)
        value = dot(place, dot(rows, wv_v[:, columns]).astype(BF)).reshape(16, 24, 256)
        kv_s[h] = jnp.concatenate([key, value], axis=1).astype(BF)
        copies = [
            remote(kv_s.at[h, peer[0]], kv_r.at[h, dp], kv_ss.at[h, i], kv_rs.at[h, i], peer)
            for i, peer in enumerate(dp_peers)
        ]
        for copy in copies:
            copy.start()
        kv_r[h, dp] = kv_s[h, dp]
        kv_c.append(copies)
        if h == 0:
            first_g.relay()
            for s in (1, 3):
                eno_f[s].start()

    first_g.wait()
    eno_f[2].start()
    for copy in epz:
        copy.wait_recv()
    ep_g = Gather(
        ep.at[:, :, mp],
        lambda place: ep.at[:, :, place * 2 + c],
        lambda block: (block.at[0], block.at[1]),
        x,
        at_x,
        ep_ss,
        ep_rs,
    )

    def ep_forward(s):
        block = ep.at[:, :, add4(x, 4 - s) * 2 + c]
        return remote(block, block, ep_ss.at[4 + s], ep_rs.at[4 + s], sib)

    ep_f = {s: ep_forward(s) for s in range(4)}
    ep_f[0].start()

    gc_and_first()

    place_of = lax.broadcasted_iota(jnp.int32, (1, 256), 1)
    bound = jnp.int32(0)
    segment = jnp.zeros((1, 256), jnp.int32)
    for e in range(8):
        bound = bound + len_ref[0, e]
        segment = segment + jnp.where(bound <= place_of, 1, 0)
    segment = segment.astype(F32) + 1.0

    scale = DH**-0.5
    ret_c = []
    gz_g = [[], []]
    gather_at, reduce_at = [at_z, at_y], [at_y, at_z]
    gather_me, reduce_me = [z, y], [y, z]

    def gather(h, part):
        here = gather_me[h]
        g_all[h, here, :, part] = g_own[h, :, part]
        gz_g[h].append(
            Gather(
                g_own.at[h, :, part],
                lambda place: g_all.at[h, place, :, part],
                lambda block: (block.at[0:4], block.at[4:8]),
                here,
                gather_at[h],
                gz_ss.at[h, part],
                gz_rs.at[h, part],
            )
        )

    row_dot = jnp.zeros((1, 256), F32)
    for copy in ex_c:
        copy.wait_recv()
    ex = enc_all[:, 0:16, D : D + 128].reshape(128, 128).astype(F32)
    ex = jnp.concatenate([ex, ex_r[...].astype(F32)[:, 0:24, :].reshape(384, 128)], axis=0)
    allowed = jnp.concatenate([ex, ex], axis=1) == segment
    for h in range(2):
        for copy in kv_c[h]:
            copy.wait_recv()
        both = kv_r[h].astype(F32)
        key_v[h, 128:512, :] = both[:, 0:24, :].reshape(384, 256).astype(BF)
        value_v[h, 128:512, :] = both[:, 24:48, :].reshape(384, 256).astype(BF)
        key = key_v[h]
        value = value_v[h]
        raw = dot_nt(key, q_v[h])
        scores = jnp.where(allowed, raw * scale, -1e30)
        top = jnp.max(scores, axis=0, keepdims=True)
        weights = jnp.where(allowed, jnp.exp(scores - top), 0.0)
        probs = weights / jnp.sum(weights, axis=0, keepdims=True)
        grad_probs = dot_nt(value, gc_v[h])
        inner = jnp.sum(probs * grad_probs, axis=0, keepdims=True)
        grad_scores = (probs * (grad_probs - inner) * scale).astype(BF)
        row_dot = row_dot + jnp.sum(grad_scores.astype(F32) * raw, axis=0, keepdims=True)
        grad_key = dot(grad_scores, q_v[h])
        grad_value = dot(probs.astype(BF), gc_v[h])
        ret_s[h] = jnp.concatenate(
            [grad_key[128:512, :].reshape(16, 24, 256), grad_value[128:512, :].reshape(16, 24, 256)],
            axis=1,
        ).astype(BF)
        copies = [
            remote(ret_s.at[h, peer[0]], ret_r.at[h, dp], ret_ss.at[h, i], ret_rs.at[h, i], peer)
            for i, peer in enumerate(dp_peers)
        ]
        for copy in copies:
            copy.start()
        ret_c.append(copies)
        ret_r[h, dp] = ret_s[h, dp]
        g_own[h, :, 0, :, 0:256] = grad_key[0:128, :].astype(BF).reshape(8, 16, 256)
        g_own[h, :, 0, :, 256:512] = grad_value[0:128, :].astype(BF).reshape(8, 16, 256)
        gq_v[:, h * DH : (h + 1) * DH] = dot_tn(grad_scores, key).astype(BF)

    for h in range(2):
        gather(h, 0)
    rd_all[mp] = jnp.broadcast_to(row_dot, (8, 256))
    rd_c = [
        remote(rd_all.at[mp], rd_all.at[mp], rd_ss.at[i], rd_rs.at[i], peer)
        for i, peer in enumerate(mp_peers)
    ]
    for copy in rd_c:
        copy.start()

    def take_back(h):
        for copy in ret_c[h]:
            copy.wait_recv()
        both = ret_r[h].astype(F32)
        for k in range(2):
            back = both[:, k * 24 : (k + 1) * 24, :].reshape(384, 256).astype(BF)
            back = dot(place_t[...], back).astype(BF).reshape(8, 16, 256)
            g_own[h, :, 1, :, k * 256 : (k + 1) * 256] = back
        gather(h, 1)

    def row_halves(block):
        return block.at[0:128], block.at[128:256]

    def column_halves(block):
        return block.at[:, 0 : D // 2], block.at[:, D // 2 : D]

    @pl.loop(0, 4)
    def _(i):
        for k in range(2):
            rows = pl.ds(pl.multiple_of((i * 2 + k) * 512, 512), 512)
            gn_t[i, k] = dot_nt(gq_v[...], wq_v[rows, :]).astype(BF)

    gn_pair = remote(gn_t.at[:, other], gn_sib, gn_ss.at[6], gn_rs.at[6], sib)
    gn_pair.start()

    ge_pair = []

    def enc_term(part):
        @pl.loop(0, 8)
        def _(i):
            rows = pl.ds(pl.multiple_of(i * 512, 512), 512)
            own = [g_own[h, :, part].reshape(128, 512) for h in range(2)]
            keys = jnp.concatenate([own[0][:, 0:256], own[1][:, 0:256]], axis=1)
            values = jnp.concatenate([own[0][:, 256:512], own[1][:, 256:512]], axis=1)
            total = dot_nt(keys, wk_v[rows, :]) + dot_nt(values, wv_v[rows, :])
            total = total.astype(BF).reshape(4, 2, 16, 512)
            for k in range(2):
                ge_t[part, k, :, :, rows] = total[:, k]

        pair = remote(
            ge_t.at[part, other], ge_sib.at[part], ge_ss.at[part, 6], ge_rs.at[part, 6], sib
        )
        pair.start()
        ge_pair.append(pair)

    ge_red = []

    def enc_reduce(part):
        ge_pair[part].wait_recv()

        @pl.loop(0, 4)
        def _(i):
            ge_s[part, i] = (ge_t[part, c, i].astype(F32) + ge_sib[part, i].astype(F32)).astype(BF)

        red = Reduce(
            lambda s: ge_s.at[part, add4(x, s)],
            column_halves,
            ge_q.at[part],
            ge_r.at[part],
            at_x,
            ge_ss.at[part],
            ge_rs.at[part],
        )
        red.send_far()
        red.send_near()
        ge_red.append(red)

    ep_g.relay()
    for s in (1, 3):
        ep_f[s].start()
    enc_term(0)
    gn_pair.wait_recv()

    @pl.loop(0, 4)
    def _(i):
        gn_s[i] = (gn_t[i, c].astype(F32) + gn_sib[i].astype(F32)).astype(BF)

    gn_red = Reduce(lambda s: gn_s.at[add4(x, s)], row_halves, gn_q, gn_r, at_x, gn_ss, gn_rs)
    gn_red.send_far()
    gn_red.send_near()
    take_back(0)
    enc_reduce(0)
    take_back(1)
    for h in range(2):
        gz_g[h][0].relay()
    enc_term(1)
    for h in range(2):
        gz_g[h][1].relay()
    ep_g.wait()
    ep_f[2].start()
    gn_red.relay()
    enc_reduce(1)

    for s in range(4):
        ep_f[s].wait_recv()
    for h in range(2):
        for b in range(4):
            for k in range(4):
                part = ep[h, k, :, :, b * 256 : (b + 1) * 256].reshape(256, 256)
                ep_t[h, b, :, k * 256 : (k + 1) * 256] = part.T
    ge_red[0].relay()

    gy_red = []

    def scatter(h):
        for g in gz_g[h]:
            g.wait()
        every = g_all[h].reshape(1024, 512)
        here = reduce_me[h]
        red = Reduce(
            lambda s: gw_s.at[h, s - 1],
            row_halves,
            gw_q.at[h],
            gw_r.at[h],
            reduce_at[h],
            gy_ss.at[h],
            gy_rs.at[h],
        )
        for s in (2, 1, 3):
            gw_s[h, s - 1] = dot(ep_t[h, add4(here, s)], every).astype(BF)
            if s == 2:
                red.send_far()
        red.send_near()
        own = dot(ep_t[h, here], every)
        gwk_ref[:, h * DH : (h + 1) * DH] = own[:, 0:256]
        gwv_ref[:, h * DH : (h + 1) * DH] = own[:, 256:512]
        gy_red.append(red)

    scatter(0)

    scatter(1)
    for red in gy_red:
        red.relay()
    ge_red[1].relay()

    outs = [
        pltpu.make_async_copy(src, dst, out_sem.at[i])
        for i, (src, dst) in enumerate(
            [(gd_ref, gd_hbm), (ge_ref, ge_hbm), (gwk_ref, gwk_hbm), (gwv_ref, gwv_hbm)]
        )
    ]

    total = ge_red[0].total(ge_s[0, x].astype(F32))
    back_s[...] = total.reshape(16, 32, 128).astype(BF)
    back_c = [
        remote(back_s.at[peer[0]], back_r.at[dp], back_ss.at[i], back_rs.at[i], peer)
        for i, peer in enumerate(dp_peers)
    ]
    for copy in back_c:
        copy.start()
    back_r[dp] = back_s[dp]

    for copy in rd_c:
        copy.wait_recv()
    inner = rd_all[0]
    for i in range(1, 8):
        inner = inner + rd_all[i]
    inner = jnp.broadcast_to(inner[0:1, :], (128, 256)).T * (1.0 / D)
    share = pl.ds(pl.multiple_of(mp * 512, 512), 512)
    total = gn_red.total(gn_s[x].astype(F32))
    scaled = total * gain_ref[share].astype(F32).reshape(1, 512)
    rms = rms_v[:, 0:1]
    unit = dec_v[:, share].astype(F32) / rms
    gd_ref[...] = ((scaled - unit * inner[:, 0:1]) / rms).astype(BF)
    outs[0].start()

    for h in range(2):
        columns = slice(h * DH, (h + 1) * DH)
        own = jnp.concatenate([gwk_ref[:, columns], gwv_ref[:, columns]], axis=1)
        total = gy_red[h].total(own)
        gwk_ref[:, columns] = total[:, 0:256]
        gwv_ref[:, columns] = total[:, 256:512]

    outs[2].start()
    outs[3].start()
    last = ge_red[1].total(ge_s[1, x].astype(F32)).astype(BF)
    for copy in back_c:
        copy.wait_recv()
    rows = back_r[...].astype(F32).reshape(16, D).astype(BF)
    rows = jnp.concatenate([rows, last], axis=0)
    ge_ref[...] = dot_tn(perm_v[:, 0:32].astype(BF), rows).astype(BF)
    outs[1].start()
    finish()
    for copy in outs:
        copy.wait()


def hand_on(a, b, c, d, a_out, b_out, c_out, d_out, a_v, b_v, c_v, d_v, sem):
    into = [(c, c_v), (d, d_v), (a, a_v), (b, b_v)]
    out = [(c_v, c_out), (d_v, d_out), (a_v, a_out), (b_v, b_out)]
    into = [pltpu.make_async_copy(src, dst, sem.at[0, i]) for i, (src, dst) in enumerate(into)]
    out = [pltpu.make_async_copy(src, dst, sem.at[1, i]) for i, (src, dst) in enumerate(out)]
    for copy in into:
        copy.start()
    for first, second in zip(into, out):
        first.wait()
        second.start()
    for copy in out:
        copy.wait()


def local(
    enc,
    enc_owner,
    enc_example,
    dec,
    dec_lengths,
    norm_gain,
    w_query,
    w_key,
    w_value,
    w_out,
    grad_out,
):
    vmem = pl.BlockSpec(memory_space=pltpu.VMEM)
    smem = pl.BlockSpec(memory_space=pltpu.SMEM)
    hbm = pl.BlockSpec(memory_space=pl.ANY)
    dma = pltpu.SemaphoreType.DMA
    V = pltpu.VMEM
    shapes = (
        jax.ShapeDtypeStruct((256, 512), BF),
        jax.ShapeDtypeStruct((32, D), BF),
        jax.ShapeDtypeStruct((256, 512), F32),
        jax.ShapeDtypeStruct((256, 512), F32),
    )
    results = pl.pallas_call(
        kernel,
        name="cross_attention_grads",
        out_shape=shapes,
        in_specs=[hbm, smem, smem, smem, vmem] + [hbm] * 6,
        out_specs=(hbm,) * 4,
        scratch_shapes=[
            V((256, 512), BF),
            V((32, D), BF),
            V((256, 512), F32),
            V((256, 512), F32),
            V((32, D), BF),
            V((256, D), BF),
            V((256, D), BF),
            V((D, 512), BF),
            V((D, 512), BF),
            V((D, 512), BF),
            V((512, D), BF),
            V((8, 32, D + 128), BF),
            V((256, D), BF),
            V((256, 128), F32),
            V((8, 8, 128), F32),
            V((2, 256, 256), BF),
            V((2, 256, 256), BF),
            V((256, 512), BF),
            V((32, 128), F32),
            V((128, 384), BF),
            V((16, 48, 128), F32),
            V((16, 48, 128), BF),
            V((16, 48, 128), BF),
            V((16, 32, 128), BF),
            V((16, 32, 128), BF),
            V((2, 16, 48, 256), BF),
            V((2, 16, 48, 256), BF),
            V((2, 512, 256), BF),
            V((2, 512, 256), BF),
            V((2, 16, 48, 256), BF),
            V((2, 16, 48, 256), BF),
            V((2, 8, 2, 16, 512), BF),
            V((2, 4, 8, 2, 16, 512), BF),
            V((2, 4, 8, 32, 1024), BF),
            V((2, 4, 256, 1024), BF),
            V((2, 3, 256, 512), BF),
            V((2, 2, 256, 512), BF),
            V((2, 2, 128, 512), BF),
            V((4, 2, 256, 512), BF),
            V((4, 256, 512), BF),
            V((4, 256, 512), BF),
            V((2, 256, 512), BF),
            V((2, 128, 512), BF),
            V((2, 2, 4, 16, D), BF),
            V((2, 4, 16, D), BF),
            V((2, 4, 16, D), BF),
            V((2, 2, 16, D), BF),
            V((2, 2, 16, D // 2), BF),
            V((16, 32, 128), BF),
            V((16, 32, 128), BF),
            V((8, 8, 256), F32),
            dma((7,)),
            dma((4,)),
            dma((15,)),
            dma((15,)),
            dma((8,)),
            dma((8,)),
            dma((8,)),
            dma((8,)),
            dma((15,)),
            dma((15,)),
            dma((7,)),
            dma((7,)),
            dma((15,)),
            dma((15,)),
            dma((10,)),
            dma((10,)),
            dma((2, 15)),
            dma((2, 15)),
            dma((2, 15)),
            dma((2, 15)),
            dma((7,)),
            dma((7,)),
            dma((7,)),
            dma((7,)),
            dma((2, 7)),
            dma((2, 7)),
            dma((2, 2, 4)),
            dma((2, 2, 4)),
            dma((2, 6)),
            dma((2, 6)),
            dma((15,)),
            dma((15,)),
        ],
        compiler_params=pltpu.CompilerParams(
            collective_id=0, has_side_effects=True, vmem_limit_bytes=60 * 1024 * 1024
        ),
    )(
        enc,
        enc_owner,
        enc_example,
        dec_lengths,
        norm_gain,
        dec,
        grad_out,
        w_query,
        w_key,
        w_value,
        w_out,
    )
    return pl.pallas_call(
        hand_on,
        name="hand_on",
        out_shape=shapes,
        in_specs=[hbm] * 4,
        out_specs=(hbm,) * 4,
        scratch_shapes=[V(shape.shape, shape.dtype) for shape in shapes] + [dma((2, 4))],
    )(*results)


def solution(mesh):
    placed = (
        P(("dp", "mp"), None),
        P(("dp", "mp")),
        P(("dp", "mp")),
        P("dp", None),
        P("dp", None),
        P(),
        P(None, "mp"),
        P(None, "mp"),
        P(None, "mp"),
        P("mp", None),
        P("dp", None),
    )
    return jax.shard_map(
        local,
        mesh=mesh,
        in_specs=placed,
        out_specs=(P("dp", "mp"), P(("dp", "mp"), None), P("dp", "mp"), P("dp", "mp")),
        check_vma=False,
    )
```

```python
import functools

import jax
import jax.numpy as jnp
from jax import lax
from jax.experimental import pallas as pl
from jax.experimental.pallas import tpu as pltpu
from jax.sharding import PartitionSpec as P

MESH = pl.DeviceIdType.MESH
BF = jnp.bfloat16
F32 = jnp.float32
DH = 256
D = 4096
NT = (((1,), (1,)), ((), ()))
TN = (((0,), (0,)), ((), ()))


def dot(a, b):
    return jnp.dot(a, b, preferred_element_type=F32)


def dot_nt(a, b):
    return lax.dot_general(a, b, NT, preferred_element_type=F32)


def dot_tn(a, b):
    return lax.dot_general(a, b, TN, preferred_element_type=F32)


class Copy:
    def __init__(self, copy, started):
        self.copy, self.started, self.received = copy, started, False

    def start(self):
        self.started.append(self)
        self.copy.start()

    def wait_recv(self):
        if not self.received:
            self.received = True
            self.copy.wait_recv()


def add4(value, step):
    return lax.rem(value + step, 4)


def kernel(
    enc_hbm,
    owner_ref,
    example_ref,
    len_ref,
    gain_ref,
    dec_hbm,
    go_hbm,
    wq_hbm,
    wk_hbm,
    wv_hbm,
    wo_hbm,
    gd_hbm,
    ge_hbm,
    gwk_hbm,
    gwv_hbm,
    gd_ref,
    ge_ref,
    gwk_ref,
    gwv_ref,
    enc_ref,
    dec_v,
    go_v,
    wq_v,
    wk_v,
    wv_v,
    wo_v,
    enc_all,
    normed,
    rms_v,
    info_all,
    q_v,
    gc_v,
    gq_v,
    perm_v,
    place_t,
    one_s,
    one_b,
    one_r,
    ex_s,
    ex_r,
    kv_s,
    kv_r,
    key_v,
    value_v,
    ret_s,
    ret_r,
    g_own,
    g_all,
    ep,
    ep_t,
    gw_s,
    gw_r,
    gw_q,
    gn_t,
    gn_sib,
    gn_s,
    gn_r,
    gn_q,
    ge_t,
    ge_sib,
    ge_s,
    ge_r,
    ge_q,
    back_s,
    back_r,
    rd_all,
    load_sem,
    out_sem,
    one_ss,
    one_rs,
    enc_ss,
    enc_rs,
    eno_ss,
    eno_rs,
    ex_ss,
    ex_rs,
    info_ss,
    info_rs,
    epz_ss,
    epz_rs,
    ep_ss,
    ep_rs,
    kv_ss,
    kv_rs,
    ret_ss,
    ret_rs,
    rd_ss,
    rd_rs,
    gn_ss,
    gn_rs,
    ge_ss,
    ge_rs,
    gz_ss,
    gz_rs,
    gy_ss,
    gy_rs,
    back_ss,
    back_rs,
):
    dp = lax.axis_index("dp")
    mp = lax.axis_index("mp")
    y, z = dp // 4, lax.rem(dp, 4)
    x, c = mp // 2, lax.rem(mp, 2)
    other = 1 - c
    sib = (dp, x * 2 + other)

    def at_x(step):
        return (dp, add4(x, step) * 2 + c)

    def at_y(step):
        return (add4(y, step) * 4 + z, mp)

    def at_z(step):
        return (y * 4 + add4(z, step), mp)

    dp_peers = [(lax.rem(dp + i, 16), mp) for i in range(1, 16)]
    mp_peers = [(dp, lax.rem(mp + i, 8)) for i in range(1, 8)]

    barrier = pltpu.get_barrier_semaphore()
    for peer in dp_peers + mp_peers:
        pl.semaphore_signal(barrier, inc=1, device_id=peer, device_id_type=MESH)

    started = []

    def remote(src, dst, ss, rs, who):
        copy = pltpu.make_async_remote_copy(
            src_ref=src, dst_ref=dst, send_sem=ss, recv_sem=rs, device_id=who, device_id_type=MESH
        )
        return Copy(copy, started)

    def finish():
        for i in range(7):
            load(i)
        for copy in started:
            copy.wait_recv()
        for copy in started:
            copy.copy.wait_send()

    class Gather:
        def __init__(self, src, slot, halves, place, at, ss, rs):
            self.slot, self.halves, self.place, self.at, self.ss, self.rs = slot, halves, place, at, ss, rs
            self.one = [remote(src, slot(place), ss.at[i], rs.at[i], at(s)) for i, s in enumerate((1, 3))]
            for copy in self.one:
                copy.start()

        def relay(self):
            self.two = []
            for i, s in enumerate((1, 3)):
                self.one[i].wait_recv()
                half = self.halves(self.slot(add4(self.place, 4 - s)))[i]
                copy = remote(half, half, self.ss.at[2 + i], self.rs.at[2 + i], self.at(s))
                copy.start()
                self.two.append(copy)

        def wait(self):
            for copy in self.two:
                copy.wait_recv()

    class Reduce:
        def __init__(self, term, halves, far, got, at, ss, rs):
            self.term, self.halves, self.far, self.got = term, halves, far, got
            self.at, self.ss, self.rs = at, ss, rs
            self.copies = []

        def send(self, src, dst, i, s):
            copy = remote(src, dst, self.ss.at[i], self.rs.at[i], self.at(s))
            copy.start()
            self.copies.append(copy)

        def send_far(self):
            for i, s in enumerate((1, 3)):
                self.send(self.halves(self.term(2))[i], self.far.at[i], i, s)

        def send_near(self):
            for i, s in enumerate((1, 3)):
                self.send(self.halves(self.term(s))[1 - i], self.halves(self.got.at[i])[1 - i], 2 + i, s)

        def relay(self):
            for i, s in enumerate((1, 3)):
                self.copies[i].wait_recv()
                half = self.halves(self.term(s))[i]
                half[...] = (half[...].astype(F32) + self.far[i].astype(F32)).astype(BF)
                self.send(half, self.halves(self.got.at[i])[i], 4 + i, s)

        def total(self, own):
            for copy in self.copies:
                copy.wait_recv()
            return own + self.got[0].astype(F32) + self.got[1].astype(F32)

    loads = [
        pltpu.make_async_copy(src, dst, load_sem.at[i])
        for i, (src, dst) in enumerate(
            [
                (dec_hbm, dec_v),
                (wq_hbm, wq_v),
                (go_hbm, go_v),
                (wo_hbm, wo_v),
                (wk_hbm, wk_v),
                (wv_hbm, wv_v),
                (enc_hbm, enc_ref),
            ]
        )
    ]
    for i in (6, 0, 1, 4, 5, 2, 3):
        loads[i].start()
    loaded = set()

    def load(i):
        if i not in loaded:
            loaded.add(i)
            loads[i].wait()

    line = lax.broadcasted_iota(jnp.int32, (8, 128), 0)
    lane = lax.broadcasted_iota(jnp.int32, (8, 128), 1)
    ids = jnp.full((8, 128), -1, jnp.int32)
    for r in range(32):
        ids = jnp.where(lane == r, jnp.where(line == 0, owner_ref[r], example_ref[r]), ids)
    ids = ids.astype(F32)
    owner = ids[0:1, :]
    example = ids[1:2, :] + 1.0
    before = lax.broadcasted_iota(jnp.int32, (128, 128), 0)
    after = lax.broadcasted_iota(jnp.int32, (128, 128), 1)
    upper = jnp.where(before < after, 1.0, 0.0).astype(BF)
    onehot = lax.broadcasted_iota(jnp.int32, (16, 128), 0).astype(F32) == owner
    onehot = jnp.where(onehot, 1.0, 0.0)
    rank = jnp.sum(dot(onehot.astype(BF), upper) * onehot, axis=0, keepdims=True)
    later = jnp.where(rank > 0.5, 1.0, 0.0)
    order = dot(jnp.broadcast_to(later, (16, 128)).astype(BF), upper)[0:1, :]
    position = jnp.where(rank > 0.5, 16.0 + order, owner)
    perm = lax.broadcasted_iota(jnp.int32, (32, 128), 0).astype(F32) == position
    perm = jnp.where(perm, 1.0, 0.0)
    perm_v[...] = perm
    perm = perm[:, 0:32].astype(BF)
    lane_of = jnp.where(rank > 0.5, order + (mp * 16).astype(F32), -1.0)
    moved = jnp.broadcast_to(lane_of, (128, 128)).T == after.astype(F32)
    moved = jnp.where(moved, 1.0, 0.0).astype(BF)
    facts = jnp.where(line == 0, owner, jnp.where(line == 1, rank, example))
    facts = jnp.concatenate([facts, facts], axis=0).astype(BF)
    info_all[mp] = dot(facts, moved)[0:8, :]
    first = jnp.sum(perm_v[0:16, :] * example, axis=1, keepdims=True)
    load(6)
    for i in range(8):
        columns = slice(i * 512, (i + 1) * 512)
        rows = dot(perm, enc_ref[:, columns])
        enc_all[mp, 16:32, columns] = rows[16:32, :].astype(BF)
        one_s[:, i * 4 : (i + 1) * 4, :] = rows[0:16, :].reshape(16, 4, 128)
    one_s[:, 32:48, :] = jnp.broadcast_to(first.reshape(16, 1, 1), (16, 16, 128))
    one_b[...] = one_s[...].astype(BF)

    pl.semaphore_wait(barrier, 22)

    def later_halves(block):
        return block.at[:, 0 : D // 2], block.at[:, D // 2 : D]

    mine = enc_all.at[mp, 16:32, 0:D]
    later_g = Gather(
        mine, lambda place: enc_all.at[place * 2 + c, 16:32, 0:D], later_halves, x, at_x, enc_ss, enc_rs
    )
    one_c = [
        remote(one_b.at[peer[0]], one_r.at[dp], one_ss.at[i], one_rs.at[i], peer)
        for i, peer in enumerate(dp_peers)
    ]
    for copy in one_c:
        copy.start()
    one_r[dp] = one_b[dp]
    info_c = [
        remote(info_all.at[mp], info_all.at[mp], info_ss.at[i], info_rs.at[i], peer)
        for i, peer in enumerate(mp_peers)
    ]
    for copy in info_c:
        copy.start()

    def enc_forward(s):
        block = enc_all.at[add4(x, 4 - s) * 2 + c, 16:32, 0:D]
        return remote(block, block, enc_ss.at[4 + s], enc_rs.at[4 + s], sib)

    enc_f = {s: enc_forward(s) for s in range(4)}
    enc_f[0].start()

    load(0)

    @pl.loop(0, 8)
    def _(i):
        rows = pl.ds(pl.multiple_of(i * 32, 32), 32)
        wide = dec_v[rows, :].astype(F32)
        rms = jnp.sqrt(jnp.mean(wide * wide, axis=-1, keepdims=True) + 1e-06)
        rms_v[rows, :] = jnp.broadcast_to(rms, (32, 128))
        normed[rows, :] = ((wide * (1.0 / rms)) * gain_ref[...].astype(F32).reshape(1, D)).astype(BF)

    load(1)
    for h in range(2):
        q_v[h] = dot(normed[...], wq_v[:, h * DH : (h + 1) * DH]).astype(BF)
    later_g.relay()
    for s in (1, 3):
        enc_f[s].start()
    for copy in one_c:
        copy.wait_recv()
    rows = one_r[...].astype(F32)
    enc_all[mp, 0:16, 0:D] = rows[:, 0:32, :].reshape(16, D).astype(BF)
    enc_all[mp, 0:16, D : D + 128] = rows[:, 32, :].astype(BF)
    def first_halves(block):
        return block.at[:, 0 : D // 2], block.at[:, D // 2 : D + 128]

    first_g = Gather(
        enc_all.at[mp, 0:16, :],
        lambda place: enc_all.at[place * 2 + c, 0:16, :],
        first_halves,
        x,
        at_x,
        eno_ss,
        eno_rs,
    )

    def eno_forward(s):
        block = enc_all.at[add4(x, 4 - s) * 2 + c, 0:16, :]
        return remote(block, block, eno_ss.at[4 + s], eno_rs.at[4 + s], sib)

    eno_f = {s: eno_forward(s) for s in range(4)}
    eno_f[0].start()
    epz = []
    for s in (1, 2, 3):
        for b in range(4):
            column = pl.multiple_of((b * 4 + add4(z, s)) * 256, 256)
            epz.append(
                remote(
                    enc_all.at[mp, :, pl.ds(column, 256)],
                    ep.at[0, z, mp, :, pl.ds(b * 256, 256)],
                    epz_ss.at[(s - 1) * 4 + b],
                    epz_rs.at[(s - 1) * 4 + b],
                    at_z(s),
                )
            )
        column = pl.multiple_of(add4(y, s) * 1024, 1024)
        epz.append(
            remote(
                enc_all.at[mp, :, pl.ds(column, 1024)],
                ep.at[1, y, mp],
                epz_ss.at[11 + s],
                epz_rs.at[11 + s],
                at_y(s),
            )
        )
    for copy in epz:
        copy.start()
    for b in range(4):
        column = pl.multiple_of((b * 4 + z) * 256, 256)
        ep[0, z, mp, :, pl.ds(b * 256, 256)] = enc_all[mp, :, pl.ds(column, 256)]
    ep[1, y, mp] = enc_all[mp, :, pl.ds(pl.multiple_of(y * 1024, 1024), 1024)]

    def gc_and_first():
        load(2)
        load(3)
        for h in range(2):
            gc_v[h] = dot_nt(go_v[...], wo_v[h * DH : (h + 1) * DH, :]).astype(BF)
        for s in range(4):
            eno_f[s].wait_recv()
        rows = enc_all[:, 0:16, 0:D].reshape(128, D)
        for h in range(2):
            columns = slice(h * DH, (h + 1) * DH)
            key_v[h, 0:128, :] = dot(rows, wk_v[:, columns]).astype(BF)
            value_v[h, 0:128, :] = dot(rows, wv_v[:, columns]).astype(BF)

    for copy in info_c:
        copy.wait_recv()
    info = info_all[0]
    for i in range(1, 8):
        info = info + info_all[i]
    block = lax.shift_right_logical(lax.broadcasted_iota(jnp.int32, (1, 128), 1), 4).astype(F32)
    target = info[0:1, :] * 24.0 + block * 3.0 + info[1:2, :] - 1.0
    slot_id = lax.broadcasted_iota(jnp.int32, (384, 128), 0).astype(F32)
    placed = jnp.where(slot_id == target, 1.0, 0.0)
    place = placed.astype(BF)
    place_t[...] = placed.T.astype(BF)
    slot_example = jnp.sum(placed * info[2:3, :], axis=1, keepdims=True)
    slot_example = jnp.broadcast_to(slot_example, (384, 128)).reshape(16, 24, 128)
    ex_s[...] = jnp.concatenate([slot_example, jnp.zeros((16, 8, 128), F32)], axis=1).astype(BF)
    ex_c = [
        remote(ex_s.at[peer[0]], ex_r.at[dp], ex_ss.at[i], ex_rs.at[i], peer)
        for i, peer in enumerate(dp_peers)
    ]
    for copy in ex_c:
        copy.start()
    ex_r[dp] = ex_s[dp]

    later_g.wait()
    enc_f[2].start()
    for s in range(4):
        enc_f[s].wait_recv()
    load(4)
    load(5)
    kv_c = []
    for h in range(2):
        columns = slice(h * DH, (h + 1) * DH)
        rows = enc_all[:, 16:32, 0:D].reshape(128, D)
        key = dot(place, dot(rows, wk_v[:, columns]).astype(BF)).reshape(16, 24, 256)
        value = dot(place, dot(rows, wv_v[:, columns]).astype(BF)).reshape(16, 24, 256)
        kv_s[h] = jnp.concatenate([key, value], axis=1).astype(BF)
        copies = [
            remote(kv_s.at[h, peer[0]], kv_r.at[h, dp], kv_ss.at[h, i], kv_rs.at[h, i], peer)
            for i, peer in enumerate(dp_peers)
        ]
        for copy in copies:
            copy.start()
        kv_r[h, dp] = kv_s[h, dp]
        kv_c.append(copies)
        if h == 0:
            first_g.relay()
            for s in (1, 3):
                eno_f[s].start()

    first_g.wait()
    eno_f[2].start()
    for copy in epz:
        copy.wait_recv()
    ep_g = Gather(
        ep.at[:, :, mp],
        lambda place: ep.at[:, :, place * 2 + c],
        lambda block: (block.at[0], block.at[1]),
        x,
        at_x,
        ep_ss,
        ep_rs,
    )

    def ep_forward(s):
        block = ep.at[:, :, add4(x, 4 - s) * 2 + c]
        return remote(block, block, ep_ss.at[4 + s], ep_rs.at[4 + s], sib)

    ep_f = {s: ep_forward(s) for s in range(4)}
    ep_f[0].start()

    gc_and_first()

    place_of = lax.broadcasted_iota(jnp.int32, (1, 256), 1)
    bound = jnp.int32(0)
    segment = jnp.zeros((1, 256), jnp.int32)
    for e in range(8):
        bound = bound + len_ref[0, e]
        segment = segment + jnp.where(bound <= place_of, 1, 0)
    segment = segment.astype(F32) + 1.0

    scale = DH**-0.5
    ret_c = []
    gz_g = [[], []]
    gather_at, reduce_at = [at_z, at_y], [at_y, at_z]
    gather_me, reduce_me = [z, y], [y, z]

    def gather(h, part):
        here = gather_me[h]
        g_all[h, here, :, part] = g_own[h, :, part]
        gz_g[h].append(
            Gather(
                g_own.at[h, :, part],
                lambda place: g_all.at[h, place, :, part],
                lambda block: (block.at[0:4], block.at[4:8]),
                here,
                gather_at[h],
                gz_ss.at[h, part],
                gz_rs.at[h, part],
            )
        )

    row_dot = jnp.zeros((1, 256), F32)
    for copy in ex_c:
        copy.wait_recv()
    ex = enc_all[:, 0:16, D : D + 128].reshape(128, 128).astype(F32)
    ex = jnp.concatenate([ex, ex_r[...].astype(F32)[:, 0:24, :].reshape(384, 128)], axis=0)
    allowed = jnp.concatenate([ex, ex], axis=1) == segment
    for h in range(2):
        for copy in kv_c[h]:
            copy.wait_recv()
        both = kv_r[h].astype(F32)
        key_v[h, 128:512, :] = both[:, 0:24, :].reshape(384, 256).astype(BF)
        value_v[h, 128:512, :] = both[:, 24:48, :].reshape(384, 256).astype(BF)
        key = key_v[h]
        value = value_v[h]
        raw = dot_nt(key, q_v[h])
        scores = jnp.where(allowed, raw * scale, -1e30)
        top = jnp.max(scores, axis=0, keepdims=True)
        weights = jnp.where(allowed, jnp.exp(scores - top), 0.0)
        probs = weights / jnp.sum(weights, axis=0, keepdims=True)
        grad_probs = dot_nt(value, gc_v[h])
        inner = jnp.sum(probs * grad_probs, axis=0, keepdims=True)
        grad_scores = (probs * (grad_probs - inner) * scale).astype(BF)
        row_dot = row_dot + jnp.sum(grad_scores.astype(F32) * raw, axis=0, keepdims=True)
        grad_key = dot(grad_scores, q_v[h])
        grad_value = dot(probs.astype(BF), gc_v[h])
        ret_s[h] = jnp.concatenate(
            [grad_key[128:512, :].reshape(16, 24, 256), grad_value[128:512, :].reshape(16, 24, 256)],
            axis=1,
        ).astype(BF)
        copies = [
            remote(ret_s.at[h, peer[0]], ret_r.at[h, dp], ret_ss.at[h, i], ret_rs.at[h, i], peer)
            for i, peer in enumerate(dp_peers)
        ]
        for copy in copies:
            copy.start()
        ret_c.append(copies)
        ret_r[h, dp] = ret_s[h, dp]
        g_own[h, :, 0, :, 0:256] = grad_key[0:128, :].astype(BF).reshape(8, 16, 256)
        g_own[h, :, 0, :, 256:512] = grad_value[0:128, :].astype(BF).reshape(8, 16, 256)
        gq_v[:, h * DH : (h + 1) * DH] = dot_tn(grad_scores, key).astype(BF)

    for h in range(2):
        gather(h, 0)
    rd_all[mp] = jnp.broadcast_to(row_dot, (8, 256))
    rd_c = [
        remote(rd_all.at[mp], rd_all.at[mp], rd_ss.at[i], rd_rs.at[i], peer)
        for i, peer in enumerate(mp_peers)
    ]
    for copy in rd_c:
        copy.start()

    def take_back(h):
        for copy in ret_c[h]:
            copy.wait_recv()
        both = ret_r[h].astype(F32)
        for k in range(2):
            back = both[:, k * 24 : (k + 1) * 24, :].reshape(384, 256).astype(BF)
            back = dot(place_t[...], back).astype(BF).reshape(8, 16, 256)
            g_own[h, :, 1, :, k * 256 : (k + 1) * 256] = back
        gather(h, 1)

    def row_halves(block):
        return block.at[0:128], block.at[128:256]

    def column_halves(block):
        return block.at[:, 0 : D // 2], block.at[:, D // 2 : D]

    @pl.loop(0, 4)
    def _(i):
        for k in range(2):
            rows = pl.ds(pl.multiple_of((i * 2 + k) * 512, 512), 512)
            gn_t[i, k] = dot_nt(gq_v[...], wq_v[rows, :]).astype(BF)

    gn_pair = remote(gn_t.at[:, other], gn_sib, gn_ss.at[6], gn_rs.at[6], sib)
    gn_pair.start()

    ge_pair = []

    def enc_term(part):
        @pl.loop(0, 8)
        def _(i):
            rows = pl.ds(pl.multiple_of(i * 512, 512), 512)
            own = [g_own[h, :, part].reshape(128, 512) for h in range(2)]
            keys = jnp.concatenate([own[0][:, 0:256], own[1][:, 0:256]], axis=1)
            values = jnp.concatenate([own[0][:, 256:512], own[1][:, 256:512]], axis=1)
            total = dot_nt(keys, wk_v[rows, :]) + dot_nt(values, wv_v[rows, :])
            total = total.astype(BF).reshape(4, 2, 16, 512)
            for k in range(2):
                ge_t[part, k, :, :, rows] = total[:, k]

        pair = remote(
            ge_t.at[part, other], ge_sib.at[part], ge_ss.at[part, 6], ge_rs.at[part, 6], sib
        )
        pair.start()
        ge_pair.append(pair)

    ge_red = []

    def enc_reduce(part):
        ge_pair[part].wait_recv()

        @pl.loop(0, 4)
        def _(i):
            ge_s[part, i] = (ge_t[part, c, i].astype(F32) + ge_sib[part, i].astype(F32)).astype(BF)

        red = Reduce(
            lambda s: ge_s.at[part, add4(x, s)],
            column_halves,
            ge_q.at[part],
            ge_r.at[part],
            at_x,
            ge_ss.at[part],
            ge_rs.at[part],
        )
        red.send_far()
        red.send_near()
        ge_red.append(red)

    ep_g.relay()
    for s in (1, 3):
        ep_f[s].start()
    enc_term(0)
    gn_pair.wait_recv()

    @pl.loop(0, 4)
    def _(i):
        gn_s[i] = (gn_t[i, c].astype(F32) + gn_sib[i].astype(F32)).astype(BF)

    gn_red = Reduce(lambda s: gn_s.at[add4(x, s)], row_halves, gn_q, gn_r, at_x, gn_ss, gn_rs)
    gn_red.send_far()
    gn_red.send_near()
    take_back(0)
    enc_reduce(0)
    take_back(1)
    for h in range(2):
        gz_g[h][0].relay()
    enc_term(1)
    for h in range(2):
        gz_g[h][1].relay()
    ep_g.wait()
    ep_f[2].start()
    gn_red.relay()
    enc_reduce(1)

    for s in range(4):
        ep_f[s].wait_recv()
    for h in range(2):
        for b in range(4):
            for k in range(4):
                part = ep[h, k, :, :, b * 256 : (b + 1) * 256].reshape(256, 256)
                ep_t[h, b, :, k * 256 : (k + 1) * 256] = part.T
    ge_red[0].relay()

    gy_red = []

    def scatter(h):
        for g in gz_g[h]:
            g.wait()
        every = g_all[h].reshape(1024, 512)
        here = reduce_me[h]
        red = Reduce(
            lambda s: gw_s.at[h, s - 1],
            row_halves,
            gw_q.at[h],
            gw_r.at[h],
            reduce_at[h],
            gy_ss.at[h],
            gy_rs.at[h],
        )
        for s in (2, 1, 3):
            gw_s[h, s - 1] = dot(ep_t[h, add4(here, s)], every).astype(BF)
            if s == 2:
                red.send_far()
        red.send_near()
        own = dot(ep_t[h, here], every)
        gwk_ref[:, h * DH : (h + 1) * DH] = own[:, 0:256]
        gwv_ref[:, h * DH : (h + 1) * DH] = own[:, 256:512]
        gy_red.append(red)

    scatter(0)

    scatter(1)
    for red in gy_red:
        red.relay()
    ge_red[1].relay()

    outs = [
        pltpu.make_async_copy(src, dst, out_sem.at[i])
        for i, (src, dst) in enumerate(
            [(gd_ref, gd_hbm), (ge_ref, ge_hbm)]
            + [
                (ref.at[:, h * DH : (h + 1) * DH], hbm.at[:, h * DH : (h + 1) * DH])
                for h in range(2)
                for ref, hbm in ((gwk_ref, gwk_hbm), (gwv_ref, gwv_hbm))
            ]
        )
    ]

    total = ge_red[0].total(ge_s[0, x].astype(F32))
    back_s[...] = total.reshape(16, 32, 128).astype(BF)
    back_c = [
        remote(back_s.at[peer[0]], back_r.at[dp], back_ss.at[i], back_rs.at[i], peer)
        for i, peer in enumerate(dp_peers)
    ]
    for copy in back_c:
        copy.start()
    back_r[dp] = back_s[dp]

    for copy in rd_c:
        copy.wait_recv()
    inner = rd_all[0]
    for i in range(1, 8):
        inner = inner + rd_all[i]
    inner = jnp.broadcast_to(inner[0:1, :], (128, 256)).T * (1.0 / D)
    share = pl.ds(pl.multiple_of(mp * 512, 512), 512)
    total = gn_red.total(gn_s[x].astype(F32))
    scaled = total * gain_ref[share].astype(F32).reshape(1, 512)
    rms = rms_v[:, 0:1]
    unit = dec_v[:, share].astype(F32) / rms
    gd_ref[...] = ((scaled - unit * inner[:, 0:1]) / rms).astype(BF)
    outs[0].start()

    for h in range(2):
        columns = slice(h * DH, (h + 1) * DH)
        own = jnp.concatenate([gwk_ref[:, columns], gwv_ref[:, columns]], axis=1)
        total = gy_red[h].total(own)
        gwk_ref[:, columns] = total[:, 0:256]
        gwv_ref[:, columns] = total[:, 256:512]
        outs[2 + 2 * h].start()
        outs[3 + 2 * h].start()
        if h == 0:
            last = ge_red[1].total(ge_s[1, x].astype(F32)).astype(BF)
            for copy in back_c:
                copy.wait_recv()
            rows = back_r[...].astype(F32).reshape(16, D).astype(BF)
            rows = jnp.concatenate([rows, last], axis=0)
            ge_ref[...] = dot_tn(perm_v[:, 0:32].astype(BF), rows).astype(BF)
            outs[1].start()

    finish()
    for copy in outs:
        copy.wait()


def hand_on(a, b, c, d, a_out, b_out, c_out, d_out, a_v, b_v, c_v, d_v, sem):
    into = [(c, c_v), (d, d_v), (a, a_v), (b, b_v)]
    out = [(c_v, c_out), (d_v, d_out), (a_v, a_out), (b_v, b_out)]
    into = [pltpu.make_async_copy(src, dst, sem.at[0, i]) for i, (src, dst) in enumerate(into)]
    out = [pltpu.make_async_copy(src, dst, sem.at[1, i]) for i, (src, dst) in enumerate(out)]
    for copy in into:
        copy.start()
    for first, second in zip(into, out):
        first.wait()
        second.start()
    for copy in out:
        copy.wait()


def local(
    enc,
    enc_owner,
    enc_example,
    dec,
    dec_lengths,
    norm_gain,
    w_query,
    w_key,
    w_value,
    w_out,
    grad_out,
):
    vmem = pl.BlockSpec(memory_space=pltpu.VMEM)
    smem = pl.BlockSpec(memory_space=pltpu.SMEM)
    hbm = pl.BlockSpec(memory_space=pl.ANY)
    dma = pltpu.SemaphoreType.DMA
    V = pltpu.VMEM
    shapes = (
        jax.ShapeDtypeStruct((256, 512), BF),
        jax.ShapeDtypeStruct((32, D), BF),
        jax.ShapeDtypeStruct((256, 512), F32),
        jax.ShapeDtypeStruct((256, 512), F32),
    )
    results = pl.pallas_call(
        kernel,
        name="cross_attention_grads",
        out_shape=shapes,
        in_specs=[hbm, smem, smem, smem, vmem] + [hbm] * 6,
        out_specs=(hbm,) * 4,
        scratch_shapes=[
            V((256, 512), BF),
            V((32, D), BF),
            V((256, 512), F32),
            V((256, 512), F32),
            V((32, D), BF),
            V((256, D), BF),
            V((256, D), BF),
            V((D, 512), BF),
            V((D, 512), BF),
            V((D, 512), BF),
            V((512, D), BF),
            V((8, 32, D + 128), BF),
            V((256, D), BF),
            V((256, 128), F32),
            V((8, 8, 128), F32),
            V((2, 256, 256), BF),
            V((2, 256, 256), BF),
            V((256, 512), BF),
            V((32, 128), F32),
            V((128, 384), BF),
            V((16, 48, 128), F32),
            V((16, 48, 128), BF),
            V((16, 48, 128), BF),
            V((16, 32, 128), BF),
            V((16, 32, 128), BF),
            V((2, 16, 48, 256), BF),
            V((2, 16, 48, 256), BF),
            V((2, 512, 256), BF),
            V((2, 512, 256), BF),
            V((2, 16, 48, 256), BF),
            V((2, 16, 48, 256), BF),
            V((2, 8, 2, 16, 512), BF),
            V((2, 4, 8, 2, 16, 512), BF),
            V((2, 4, 8, 32, 1024), BF),
            V((2, 4, 256, 1024), BF),
            V((2, 3, 256, 512), BF),
            V((2, 2, 256, 512), BF),
            V((2, 2, 128, 512), BF),
            V((4, 2, 256, 512), BF),
            V((4, 256, 512), BF),
            V((4, 256, 512), BF),
            V((2, 256, 512), BF),
            V((2, 128, 512), BF),
            V((2, 2, 4, 16, D), BF),
            V((2, 4, 16, D), BF),
            V((2, 4, 16, D), BF),
            V((2, 2, 16, D), BF),
            V((2, 2, 16, D // 2), BF),
            V((16, 32, 128), BF),
            V((16, 32, 128), BF),
            V((8, 8, 256), F32),
            dma((7,)),
            dma((6,)),
            dma((15,)),
            dma((15,)),
            dma((8,)),
            dma((8,)),
            dma((8,)),
            dma((8,)),
            dma((15,)),
            dma((15,)),
            dma((7,)),
            dma((7,)),
            dma((15,)),
            dma((15,)),
            dma((10,)),
            dma((10,)),
            dma((2, 15)),
            dma((2, 15)),
            dma((2, 15)),
            dma((2, 15)),
            dma((7,)),
            dma((7,)),
            dma((7,)),
            dma((7,)),
            dma((2, 7)),
            dma((2, 7)),
            dma((2, 2, 4)),
            dma((2, 2, 4)),
            dma((2, 6)),
            dma((2, 6)),
            dma((15,)),
            dma((15,)),
        ],
        compiler_params=pltpu.CompilerParams(
            collective_id=0, has_side_effects=True, vmem_limit_bytes=60 * 1024 * 1024
        ),
    )(
        enc,
        enc_owner,
        enc_example,
        dec_lengths,
        norm_gain,
        dec,
        grad_out,
        w_query,
        w_key,
        w_value,
        w_out,
    )
    return pl.pallas_call(
        hand_on,
        name="hand_on",
        out_shape=shapes,
        in_specs=[hbm] * 4,
        out_specs=(hbm,) * 4,
        scratch_shapes=[V(shape.shape, shape.dtype) for shape in shapes] + [dma((2, 4))],
    )(*results)


def solution(mesh):
    placed = (
        P(("dp", "mp"), None),
        P(("dp", "mp")),
        P(("dp", "mp")),
        P("dp", None),
        P("dp", None),
        P(),
        P(None, "mp"),
        P(None, "mp"),
        P(None, "mp"),
        P("mp", None),
        P("dp", None),
    )
    return jax.shard_map(
        local,
        mesh=mesh,
        in_specs=placed,
        out_specs=(P("dp", "mp"), P(("dp", "mp"), None), P("dp", "mp"), P("dp", "mp")),
        check_vma=False,
    )
```
